256 devices in a mesh: row: 8 (over x, z_lo), col: 32 (over z_hi, y, core).
Axes of the slice: x: 4, y: 4, z: 8 (z_hi: 4, z_lo: 2; z = z_hi * 2 + z_lo), core: 2. Of those that a mesh axis runs over, the one named last changes fastest.
Arguments:
- features: bfloat16 [65536, 256], P(('row', 'col')), may hold values from -6 to 6
- cotangent: bfloat16 [65536, 256], P(('row', 'col')), may hold values from -6 to 6
- weight: bfloat16 [256, 256], replicated, may hold values from -0.375 to 0.375
- bias: float32 [256], replicated, may hold values from -3 to 3
- adjacency: bfloat16 [8, 6144, 128, 128], P('row', 'col'), may hold values from -0.078125 to 0.078125
- tile_rows: int32 [8, 6144], P('row', 'col'), may hold values from 0 to 63
- tile_cols: int32 [8, 6144], P('row', 'col'), may hold values from 0 to 15
- live_tiles: int32 [8, 32], P('row', 'col'), may hold values from 24 to 192, as said below
Outputs:
- layer_out: bfloat16 [65536, 256], P(('row', 'col'))
- features_grad: bfloat16 [65536, 256], P(('row', 'col'))
- weight_grad: float32 [256, 256], replicated
- bias_grad: float32 [256], replicated
The draws below stay inside these ranges and needn't reach their ends.
Inputs may be any that keep to these rules, and one draw needn't show every extreme that they name: `live_tiles`: each value is 192, 96, 48 or 24, and some block has 192.
All inputs are finite; a program needn't handle non-finite values.
Results may differ from the reference program's by a relative error of at most 0.025.
Values may be sent and summed in bfloat16 or wider, within the bound.
No kernel may reach another device: no remote copies, remote signals or barrier semaphores. Data moves between devices by JAX's collectives and lax.ppermute only.
A program may use at most 128 MiB of HBM per device.

```python
import math
import jax
import jax.numpy as jnp
import numpy as np
from jax import lax

F = 256
TILE = 128
TILE_BLOCK = 64
VTX_DEV = 256
TILES_DEV = 192
GRID_ROW = 8
GRID_COL = 32
SLOTS = 6144
NV = 65536
ROW_TILES = 64
COL_TILES = 16
N_ROW = 8
N_COL = 32


def draw_live_tiles(key, part):
    key = jax.random.fold_in(key, 7)
    first_key, second_key = jax.random.split(key)
    shifts = jax.random.randint(first_key, (GRID_ROW * GRID_COL,), 0, 4)
    divisors = jnp.left_shift(jnp.ones_like(shifts), shifts)
    counts = TILES_DEV // divisors
    fullest = jax.random.randint(second_key, (), 0, GRID_ROW * GRID_COL)
    positions = jnp.arange(GRID_ROW * GRID_COL, dtype=jnp.int32)
    counts = jnp.where(positions == fullest, TILES_DEV, counts)
    return counts.reshape(GRID_ROW, GRID_COL).astype(jnp.int32)


def place_ends(entries, rng, low, top_value):
    longest = entries.shape.index(max(entries.shape))
    spots = []
    for shift in (0, 1):
        where = [jax.random.randint(jax.random.fold_in(rng, axis), (), 0, length) for axis, length in enumerate(entries.shape)]
        where[longest] = (where[longest] + shift) % entries.shape[longest]
        spots.append(tuple(where))
    return entries.at[spots[0]].set(low).at[spots[1]].set(top_value)


def shard_levels(own_key, dims, cuts, smallest, high):
    factor_of, own = 1.0, jax.random.fold_in(own_key, 6)
    for position, blocks in cuts:
        heights = jnp.exp(jax.random.uniform(jax.random.fold_in(own, position), (blocks,), jnp.float32, smallest / len(cuts), high / len(cuts)))
        factor_of = factor_of * jnp.repeat(heights, dims[position] // blocks).reshape([-1 if axis == position else 1 for axis in range(len(dims))])
    return factor_of


def rank_bounds(number_of, skew):
    loads = [(1 << 20) // math.isqrt(standing ** skew) + 1 for standing in range(1, number_of + 1)]
    width = 1 + sum(loads) // (1 << 30)
    return np.cumsum(np.array([max(1, weight // width) for weight in loads]))


def ranked_ids(rng, extent, amount, slope):
    table = rank_bounds(amount, slope)
    ticket = jax.random.randint(jax.random.fold_in(rng, 1), extent, 0, int(table[amount - 1]))
    standing = jnp.searchsorted(jnp.asarray(table, jnp.int32), ticket, side="right")
    return jax.random.permutation(jax.random.fold_in(rng, 2), amount)[standing].astype(jnp.int32)


def noise(rng, extent, scale, bound, cuts=(), kind=jnp.bfloat16):
    gain = shard_levels(rng, extent, cuts, -0.22, 0.18) if cuts else 1.0
    result = jax.random.normal(rng, extent, jnp.float32) * scale * gain
    return jnp.minimum(jnp.maximum(result, -bound), bound).astype(kind)


def setup_inputs(seed: int = 0) -> dict:
    streams_of = jax.random.split(jax.random.key(seed), 9)
    return {
        "features": noise(streams_of[0], (NV, F), 1.0, 6.0, ((0, 256),)),
        "cotangent": noise(streams_of[1], (NV, F), 1.0, 6.0, ((0, 256),)),
        "weight": noise(streams_of[2], (F, F), F ** -0.5, 0.375),
        "bias": noise(streams_of[3], (F,), 0.5, 3.0, (), jnp.float32),
        "adjacency": noise(streams_of[4], (GRID_ROW, SLOTS, TILE, TILE), (TILES_DEV * TILE * TILE // (2 * VTX_DEV)) ** -0.5, 0.078125, ((0, 8), (1, 32))),
        "tile_rows": place_ends(ranked_ids(streams_of[5], (GRID_ROW, SLOTS), ROW_TILES, 1), jax.random.fold_in(streams_of[5], 3), 0, ROW_TILES - 1).astype(jnp.int32),
        "tile_cols": place_ends(jax.random.randint(streams_of[6], (GRID_ROW, SLOTS), 0, COL_TILES), jax.random.fold_in(streams_of[6], 1), 0, COL_TILES - 1).astype(jnp.int32),
        "live_tiles": draw_live_tiles(jax.random.fold_in(streams_of[8], 71), 0),
    }


GELU_ROOT = 0.7978845608028654
GELU_CUBIC = 0.044715

def gelu_value(shifted):
    return 0.5 * shifted * (1.0 + jnp.tanh(GELU_ROOT * (shifted + GELU_CUBIC * shifted * shifted * shifted)))

def gelu_slope(shifted):
    tanh_term = jnp.tanh(GELU_ROOT * (shifted + GELU_CUBIC * shifted * shifted * shifted))
    return 0.5 * (1.0 + tanh_term) + 0.5 * shifted * (1.0 - tanh_term * tanh_term) * GELU_ROOT * (1.0 + 3.0 * GELU_CUBIC * shifted * shifted)

def tile_sum(device_tiles, take_ids, put_ids, live_count, sources, segments, transposed):
    slot_ids = jnp.arange(TILES_DEV, dtype=jnp.int32)

    def one_block(running, first_slot):
        tile_block = lax.dynamic_slice_in_dim(device_tiles, first_slot, TILE_BLOCK, 0).astype(jnp.float32)
        alive_mask = (lax.dynamic_slice_in_dim(slot_ids, first_slot, TILE_BLOCK, 0) < live_count).astype(jnp.float32)
        picked = jnp.take(sources, lax.dynamic_slice_in_dim(take_ids, first_slot, TILE_BLOCK, 0), axis=0).astype(jnp.float32)
        if transposed:
            product = jnp.einsum('tij,tif->tjf', tile_block, picked)
        else:
            product = jnp.einsum('tij,tjf->tif', tile_block, picked)
        product = product * alive_mask[:, None, None]
        targets = lax.dynamic_slice_in_dim(put_ids, first_slot, TILE_BLOCK, 0)
        return (running + jax.ops.segment_sum(product, targets, num_segments=segments), None)
    block_starts = jnp.arange(0, TILES_DEV, TILE_BLOCK, dtype=jnp.int32)
    running, _ = lax.scan(one_block, jnp.zeros((segments, TILE, F), jnp.float32), block_starts)
    return running

def column_view(full_array):
    viewed = full_array.reshape(N_ROW, N_COL, VTX_DEV // TILE, TILE, F)
    viewed = jnp.transpose(viewed, (1, 0, 2, 3, 4))
    return viewed.reshape(N_COL, COL_TILES, TILE, F)

def column_restore(viewed):
    restored = viewed.reshape(N_COL, N_ROW, VTX_DEV // TILE, TILE, F)
    restored = jnp.transpose(restored, (1, 0, 2, 3, 4))
    return restored.reshape(NV, F)

def device_pieces(adjacency, tile_rows, tile_cols, live_tiles, device):
    zero = jnp.int32(0)
    row_index = device // N_COL
    col_index = device % N_COL
    device_tiles = lax.dynamic_slice(adjacency, (row_index, col_index * TILES_DEV, zero, zero), (1, TILES_DEV, TILE, TILE))[0]
    row_ids = lax.dynamic_slice(tile_rows, (row_index, col_index * TILES_DEV), (1, TILES_DEV))[0]
    col_ids = lax.dynamic_slice(tile_cols, (row_index, col_index * TILES_DEV), (1, TILES_DEV))[0]
    live_count = lax.dynamic_slice(live_tiles, (row_index, col_index), (1, 1))[0, 0]
    return (row_index, col_index, device_tiles, row_ids, col_ids, live_count)

def reference(features, cotangent, weight, bias, adjacency, tile_rows, tile_cols, live_tiles):
    projected = jnp.dot(features, weight, preferred_element_type=jnp.float32).astype(jnp.bfloat16)
    column_tiles = column_view(projected)
    devices = jnp.arange(N_ROW * N_COL, dtype=jnp.int32)

    def forward(accumulated, device):
        row_index, col_index, device_tiles, row_ids, col_ids, live_count = device_pieces(adjacency, tile_rows, tile_cols, live_tiles, device)
        sources = lax.dynamic_index_in_dim(column_tiles, col_index, 0, keepdims=False)
        partial_value = tile_sum(device_tiles, col_ids, row_ids, live_count, sources, ROW_TILES, False)
        partial_value = lax.optimization_barrier(partial_value.astype(jnp.bfloat16)).astype(jnp.float32)
        previous = lax.dynamic_slice_in_dim(accumulated, row_index * ROW_TILES, ROW_TILES, 0)
        return (lax.dynamic_update_slice_in_dim(accumulated, previous + partial_value, row_index * ROW_TILES, 0), None)
    aggregated, _ = lax.scan(forward, jnp.zeros((NV // TILE, TILE, F), jnp.float32), devices)
    aggregated = aggregated.reshape(NV, F)
    shifted = aggregated + bias
    layer_out = gelu_value(shifted).astype(jnp.bfloat16)
    pre_grad = cotangent.astype(jnp.float32) * gelu_slope(shifted)
    grad_scale = 1.0 / math.sqrt(NV)
    bias_grad = lax.optimization_barrier(jnp.sum(pre_grad, axis=0)) * grad_scale
    pre_grad_b = pre_grad.astype(jnp.bfloat16).reshape(NV // TILE, TILE, F)

    def backward(accumulated, device):
        row_index, col_index, device_tiles, row_ids, col_ids, live_count = device_pieces(adjacency, tile_rows, tile_cols, live_tiles, device)
        sources = lax.dynamic_slice_in_dim(pre_grad_b, row_index * ROW_TILES, ROW_TILES, 0)
        partial_value = tile_sum(device_tiles, row_ids, col_ids, live_count, sources, COL_TILES, True)
        previous = lax.dynamic_index_in_dim(accumulated, col_index, 0, keepdims=False)
        return (lax.dynamic_update_index_in_dim(accumulated, previous + partial_value, col_index, 0), None)
    back_rows, _ = lax.scan(backward, jnp.zeros((N_COL, COL_TILES, TILE, F), jnp.float32), devices)
    column_grad = column_restore(back_rows)
    column_grad_b = column_grad.astype(jnp.bfloat16)
    features_grad = jnp.dot(column_grad_b, weight.T, preferred_element_type=jnp.float32).astype(jnp.bfloat16)
    weight_grad = jnp.dot(features.T, column_grad_b, preferred_element_type=jnp.float32) * grad_scale
    return (layer_out, features_grad, weight_grad, bias_grad)
```

```python
import functools
import math

import jax
import jax.numpy as jnp
from jax import lax
from jax.experimental import pallas as pl
from jax.experimental.pallas import tpu as pltpu
from jax.sharding import PartitionSpec as P

GELU_ROOT = 0.7978845608028654
GELU_CUBIC = 0.044715

N_X, N_ZL, N_ZH, N_Y, N_CORE = 4, 2, 4, 4, 2
N_ROW = N_X * N_ZL
N_COL = N_ZH * N_Y * N_CORE
GROUP = 24
VMEM_LIMIT = 56 * 1024 * 1024


def row_shift(value, dx, dzl):
    pairs = []
    for i in range(N_ROW):
        x, zl = divmod(i, N_ZL)
        pairs.append((i, (x + dx) % N_X * N_ZL + (zl ^ dzl)))
    return lax.ppermute(value, "row", pairs)


def col_shift(value, dzh=0, dy=0, dcore=0):
    pairs = []
    for i in range(N_COL):
        zh, y, core = i // (N_Y * N_CORE), i // N_CORE % N_Y, i % N_CORE
        pairs.append(
            (i, ((zh + dzh) % N_ZH * N_Y + (y + dy) % N_Y) * N_CORE + (core ^ dcore))
        )
    return lax.ppermute(value, "col", pairs)


def tile_kernel(transposed, n_src, n_out, live, take, put, tiles, *refs):
    sources = refs[:n_src]
    outs = refs[n_src : n_src + n_out]
    src, acc, sems = refs[n_src + n_out :]
    step = pl.program_id(0)
    per_src = src.shape[0] // n_src
    per_out = acc.shape[0] // n_out

    @pl.when(step == 0)
    def _():
        copies = [
            pltpu.make_async_copy(
                sources[k], src.at[pl.ds(k * per_src, per_src)], sems.at[k]
            )
            for k in range(n_src)
        ]
        for copy in copies:
            copy.start()

        @pl.loop(0, acc.shape[0])
        def _(i):
            acc[i] = jnp.zeros(acc.shape[1:], jnp.float32)

        for copy in copies:
            copy.wait()

    @pl.when(step * GROUP < live[0])
    def _():
        @pl.loop(0, GROUP // 8)
        def _(i):
            for j in range(8):
                k = i * 8 + j
                slot = step * GROUP + k
                product = lax.dot_general(
                    tiles[0, k],
                    src[take[slot]],
                    (((0 if transposed else 1,), (0,)), ((), ())),
                    preferred_element_type=jnp.float32,
                )
                acc[put[slot]] += product

    @pl.when(step == pl.num_programs(0) - 1)
    def _():
        for k in range(n_out):
            @pl.loop(0, per_out)
            def _(i):
                outs[k][i] = acc[k * per_out + i].astype(jnp.bfloat16)


def tile_sum(adjacency, live, take, put, sources, segments, n_out, transposed):
    slots, tile = adjacency.shape[1], adjacency.shape[2]
    width = sources[0].shape[-1]
    sources = [s.reshape(-1, tile, width) for s in sources]
    n_src = len(sources)
    total_src = sum(s.shape[0] for s in sources)
    per_out = segments // n_out

    def tile_block(i, live, take, put):
        return (0, jnp.minimum(i, live[0] // GROUP - 1), 0, 0)

    return pl.pallas_call(
        functools.partial(tile_kernel, transposed, n_src, n_out),
        grid_spec=pltpu.PrefetchScalarGridSpec(
            num_scalar_prefetch=3,
            grid=(slots // GROUP,),
            in_specs=[pl.BlockSpec((1, GROUP, tile, tile), tile_block)]
            + [pl.BlockSpec(memory_space=pl.ANY)] * n_src,
            out_specs=[
                pl.BlockSpec((per_out, tile, width), lambda i, *_: (0, 0, 0))
                for _ in range(n_out)
            ],
            scratch_shapes=[
                pltpu.VMEM((total_src, tile, width), jnp.bfloat16),
                pltpu.VMEM((segments, tile, width), jnp.float32),
                pltpu.SemaphoreType.DMA((n_src,)),
            ],
        ),
        out_shape=[
            jax.ShapeDtypeStruct((per_out, tile, width), jnp.bfloat16)
            for _ in range(n_out)
        ],
        compiler_params=pltpu.CompilerParams(vmem_limit_bytes=VMEM_LIMIT),
        cost_estimate=pl.CostEstimate(
            flops=2 * slots * tile * tile * width,
            bytes_accessed=slots * tile * tile * 2,
            transcendentals=0,
        ),
    )(live, take, put, adjacency, *sources)


def split_dot(exact, other, dims):
    high = exact.astype(jnp.bfloat16)
    low = (exact - high.astype(jnp.float32)).astype(jnp.bfloat16)
    dot = functools.partial(
        lax.dot_general, dimension_numbers=dims, preferred_element_type=jnp.float32
    )
    return dot(high, other) + dot(low, other)


def owner_chunk(place, position):
    core, y, zh = position // 16, position // 4 % 4, position % 4
    return (
        ((place[0] + zh) % N_ZH * N_Y + (place[1] + y) % N_Y) * N_CORE
        + (place[2] + core) % N_CORE
    )


def middle_kernel(place, h0, h1, h2, h3, weight, bias, cotangent, out, grad, load, term, pre):
    total = (
        h0[...].astype(jnp.float32)
        + h1[...].astype(jnp.float32)
        + h2[...].astype(jnp.float32)
        + h3[...].astype(jnp.float32)
    )
    shifted = split_dot(total, weight[...], (((1,), (0,)), ((), ()))) + bias[...]
    tanh_term = jnp.tanh(GELU_ROOT * (shifted + GELU_CUBIC * shifted * shifted * shifted))
    out[...] = (0.5 * shifted * (1.0 + tanh_term)).astype(jnp.bfloat16)
    slope = 0.5 * (1.0 + tanh_term) + 0.5 * shifted * (
        1.0 - tanh_term * tanh_term
    ) * GELU_ROOT * (1.0 + 3.0 * GELU_CUBIC * shifted * shifted)
    pre_grad = cotangent[...].astype(jnp.float32) * slope
    rounded = pre_grad.astype(jnp.bfloat16)
    grad[...] = rounded
    term[...] = split_dot(total, rounded, (((0,), (0,)), ((), ())))
    pre[...] = pre_grad
    chunk = term.shape[0] // N_COL
    for position in range(N_COL):
        rows = pl.ds(pl.multiple_of(owner_chunk(place, position) * chunk, chunk), chunk)
        load[position, :chunk] = term[rows, :]
        load[position, chunk:] = pre[rows, :]


def middle(place, pieces, weight, bias, cotangent):
    rows, width = cotangent.shape
    vmem = pl.BlockSpec(memory_space=pltpu.VMEM)
    return pl.pallas_call(
        middle_kernel,
        in_specs=[pl.BlockSpec(memory_space=pltpu.SMEM)] + [vmem] * 7,
        out_specs=[vmem] * 3,
        out_shape=[
            jax.ShapeDtypeStruct((rows, width), jnp.bfloat16),
            jax.ShapeDtypeStruct((rows, width), jnp.bfloat16),
            jax.ShapeDtypeStruct((N_COL, 2 * width // N_COL, width), jnp.float32),
        ],
        scratch_shapes=[
            pltpu.VMEM((width, width), jnp.float32),
            pltpu.VMEM((rows, width), jnp.float32),
        ],
        compiler_params=pltpu.CompilerParams(vmem_limit_bytes=VMEM_LIMIT),
    )(place, *pieces, weight, bias.reshape(1, width), cotangent)


def spread_kernel(scale, place, load, weight_grad, bias_grad):
    chunk = load.shape[1] // 2
    for position in range(N_COL):
        core, y, zh = position // 16, position // 4 % 4, position % 4
        owner = (
            ((place[0] + 4 - zh) % N_ZH * N_Y + (place[1] + 4 - y) % N_Y) * N_CORE
            + (place[2] + core) % N_CORE
        )
        rows = pl.ds(pl.multiple_of(owner * chunk, chunk), chunk)
        weight_grad[rows, :] = load[position, :chunk] * scale
    bias_grad[...] = (
        jnp.sum(jnp.sum(load[:, chunk:], axis=0), axis=0, keepdims=True) * scale
    )


def spread(place, load, scale):
    width = load.shape[-1]
    chunk = load.shape[1] // 2
    vmem = pl.BlockSpec(memory_space=pltpu.VMEM)
    return pl.pallas_call(
        functools.partial(spread_kernel, scale),
        in_specs=[pl.BlockSpec(memory_space=pltpu.SMEM), vmem],
        out_specs=[vmem] * 2,
        out_shape=[
            jax.ShapeDtypeStruct((N_COL * chunk, width), jnp.float32),
            jax.ShapeDtypeStruct((1, width), jnp.float32),
        ],
    )(place, load)


def last_kernel(*refs):
    *pieces, weight, out = refs
    total = pieces[0][...].astype(jnp.float32)
    for piece in pieces[1:]:
        total += piece[...].astype(jnp.float32)
    out[...] = lax.dot_general(
        total.astype(jnp.bfloat16),
        weight[...],
        (((1,), (1,)), ((), ())),
        preferred_element_type=jnp.float32,
    ).astype(jnp.bfloat16)


def last(pieces, weight):
    rows, width = pieces[0].shape
    vmem = pl.BlockSpec(memory_space=pltpu.VMEM)
    return pl.pallas_call(
        last_kernel,
        in_specs=[vmem] * (len(pieces) + 1),
        out_specs=vmem,
        out_shape=jax.ShapeDtypeStruct((rows, width), jnp.bfloat16),
    )(*pieces, weight)


def sum_over_all(load):
    kept = load[:16] + col_shift(load[16:], dcore=1)
    kept = kept[:4] + sum(
        col_shift(kept[4 * k : 4 * k + 4], dy=k) for k in range(1, N_Y)
    )
    kept = kept[0] + sum(col_shift(kept[k], dzh=k) for k in range(1, N_ZH))
    kept = kept + sum(
        row_shift(kept, dx, dzl)
        for dx in range(N_X)
        for dzl in range(N_ZL)
        if (dx, dzl) != (0, 0)
    )
    kept = jnp.stack([kept] + [col_shift(kept, dzh=k) for k in range(1, N_ZH)])
    kept = jnp.concatenate([kept] + [col_shift(kept, dy=k) for k in range(1, N_Y)])
    return jnp.concatenate([kept, col_shift(kept, dcore=1)])


def shards(features, cotangent, weight, bias, adjacency, tile_rows, tile_cols, live_tiles):
    vertices, width = features.shape
    tile = adjacency.shape[2]
    scale = 1.0 / math.sqrt(vertices * N_ROW * N_COL)
    live = live_tiles.reshape(1)
    row_id, col_id = lax.axis_index("row"), lax.axis_index("col")
    my_x, my_zl = row_id // N_ZL, row_id % N_ZL
    my_zh, my_y, my_core = col_id // 8, col_id // 2 % 4, col_id % 2
    place = jnp.stack([my_zh, my_y, my_core]).astype(jnp.int32)

    per = vertices // tile
    r, c = tile_rows[0], tile_cols[0]
    rc, cc = r // per, c // per
    r_zh, r_y, r_core = rc // 8, rc // 2 % 4, rc % 2
    c_x, c_zl = cc // 2, cc % 2
    half = (r_core ^ my_core) * 16
    put_rows = (half + ((r_y - my_y) & 3) * 4 + ((r_zh - my_zh) & 3)) * per + r % per
    take_rows = (half + ((my_y - r_y) & 3) * 4 + ((my_zh - r_zh) & 3)) * per + r % per
    put_cols = (((c_x - my_x) & 3) * 2 + (c_zl ^ my_zl)) * per + c % per
    take_cols = (((my_x - c_x) & 3) * 2 + (c_zl ^ my_zl)) * per + c % per

    moves = [(dx, dzl) for dx in range(N_X) for dzl in range(N_ZL)]
    with jax.named_scope("gather_features"):
        sources = [features] + [row_shift(features, *m) for m in moves[1:]]
    with jax.named_scope("tiles_forward"):
        parts = tile_sum(
            adjacency, live, take_cols, put_rows, sources, N_COL * per, 8, False
        )
    with jax.named_scope("sum_over_col"):
        keep, send = parts[:4], parts[4:]
        merged = [None] * 4
        for k in (2, 1, 3, 0):
            other = col_shift(send[k], dcore=1)
            merged[k] = (
                keep[k].astype(jnp.float32) + other.astype(jnp.float32)
            ).astype(jnp.bfloat16)
        arrived = [col_shift(merged[k], dy=k) for k in range(1, N_Y)]
        merged = [
            sum(
                (p[per * j : per * (j + 1)].astype(jnp.float32) for p in arrived),
                merged[0][per * j : per * (j + 1)].astype(jnp.float32),
            ).astype(jnp.bfloat16)
            for j in range(N_ZH)
        ]
        pieces = [merged[0]] + [col_shift(merged[k], dzh=k) for k in range(1, N_ZH)]
        pieces = [p.reshape(vertices, width) for p in pieces]
    with jax.named_scope("pointwise"):
        layer_out, grad, load = middle(place, pieces, weight, bias, cotangent)
    with jax.named_scope("gather_gradients"):
        own = jnp.concatenate([grad] + [col_shift(grad, dzh=k) for k in range(1, N_ZH)])
        here = [own] + [col_shift(own, dy=k) for k in range(1, N_Y)]
        there = [col_shift(p, dcore=1) for p in here]
    with jax.named_scope("sum_weight_grad"):
        weight_grad, bias_grad = spread(place, sum_over_all(load), scale)
    with jax.named_scope("tiles_backward"):
        back = tile_sum(
            adjacency, live, take_rows, put_cols, here + there, N_ROW * per, N_ROW, True
        )
    with jax.named_scope("sum_over_row"):
        back = [b.reshape(vertices, width) for b in back]
        pieces = [back[0]] + [row_shift(b, *m) for b, m in zip(back[1:], moves[1:])]
        features_grad = last(pieces, weight)
    return layer_out, features_grad, weight_grad, bias_grad.reshape(width)


def solution(mesh):
    placed = (
        P(("row", "col"), None),
        P(("row", "col"), None),
        P(),
        P(),
        P("row", "col", None, None),
        P("row", "col"),
        P("row", "col"),
        P("row", "col"),
    )
    return jax.shard_map(
        shards,
        mesh=mesh,
        in_specs=placed,
        out_specs=(P(("row", "col"), None), P(("row", "col"), None), P(), P()),
        check_vma=False,
    )
```

```python
import functools
import math

import jax
import jax.numpy as jnp
from jax import lax
from jax.experimental import pallas as pl
from jax.experimental.pallas import tpu as pltpu
from jax.sharding import PartitionSpec as P

GELU_ROOT = 0.7978845608028654
GELU_CUBIC = 0.044715

N_X, N_ZL, N_ZH, N_Y, N_CORE = 4, 2, 4, 4, 2
N_ROW = N_X * N_ZL
N_COL = N_ZH * N_Y * N_CORE
GROUP = 24
VMEM_LIMIT = 60 * 1024 * 1024
LANES = 128


def row_shift(value, dx, dzl):
    pairs = []
    for i in range(N_ROW):
        x, zl = divmod(i, N_ZL)
        pairs.append((i, (x + dx) % N_X * N_ZL + (zl ^ dzl)))
    return lax.ppermute(value, "row", pairs)


def col_shift(value, dzh=0, dy=0, dcore=0):
    pairs = []
    for i in range(N_COL):
        zh, y, core = i // (N_Y * N_CORE), i // N_CORE % N_Y, i % N_CORE
        pairs.append(
            (i, ((zh + dzh) % N_ZH * N_Y + (y + dy) % N_Y) * N_CORE + (core ^ dcore))
        )
    return lax.ppermute(value, "col", pairs)


def tile_kernel(transposed, src_sizes, out_sizes, live, take, put, tiles, *refs):
    n_src, n_out = len(src_sizes), len(out_sizes)
    sources = refs[:n_src]
    outs = refs[n_src : n_src + n_out]
    src, acc, staged, in_sems, out_sems = refs[n_src + n_out :]
    step = pl.program_id(0)

    @pl.when(step == 0)
    def _():
        copies, first = [], 0
        for k, size in enumerate(src_sizes):
            copies.append(
                pltpu.make_async_copy(
                    sources[k], src.at[pl.ds(first, size)], in_sems.at[k]
                )
            )
            first += size
        for copy in copies:
            copy.start()

        @pl.loop(0, acc.shape[0])
        def _(i):
            acc[i] = jnp.zeros(acc.shape[1:], jnp.float32)

        for copy in copies:
            copy.wait()

    @pl.when(step * GROUP < live[0])
    def _():
        @pl.loop(0, GROUP // 8)
        def _(i):
            for j in range(8):
                k = i * 8 + j
                slot = step * GROUP + k
                product = lax.dot_general(
                    tiles[0, k],
                    src[take[slot]],
                    (((0 if transposed else 1,), (0,)), ((), ())),
                    preferred_element_type=jnp.float32,
                )
                acc[put[slot]] += product

    @pl.when(step == pl.num_programs(0) - 1)
    def _():
        copies, first = [], 0
        for k, size in enumerate(out_sizes):
            start = first

            @pl.loop(0, size)
            def _(i):
                staged[start + i] = acc[start + i].astype(jnp.bfloat16)

            copies.append(
                pltpu.make_async_copy(
                    staged.at[pl.ds(start, size)], outs[k], out_sems.at[k]
                )
            )
            copies[-1].start()
            first += size
        for copy in copies:
            copy.wait()


def tile_sum(adjacency, live, take, put, sources, out_sizes, transposed):
    slots, tile = adjacency.shape[1], adjacency.shape[2]
    width = sources[0].shape[-1]
    sources = [s.reshape(-1, tile, width) for s in sources]
    src_sizes = [s.shape[0] for s in sources]

    def tile_block(i, live, take, put):
        return (0, jnp.minimum(i, live[0] // GROUP - 1), 0, 0)

    anywhere = pl.BlockSpec(memory_space=pl.ANY)
    return pl.pallas_call(
        functools.partial(tile_kernel, transposed, src_sizes, out_sizes),
        grid_spec=pltpu.PrefetchScalarGridSpec(
            num_scalar_prefetch=3,
            grid=(slots // GROUP,),
            in_specs=[pl.BlockSpec((1, GROUP, tile, tile), tile_block)]
            + [anywhere] * len(sources),
            out_specs=[anywhere] * len(out_sizes),
            scratch_shapes=[
                pltpu.VMEM((sum(src_sizes), tile, width), jnp.bfloat16),
                pltpu.VMEM((sum(out_sizes), tile, width), jnp.float32),
                pltpu.VMEM((sum(out_sizes), tile, width), jnp.bfloat16),
                pltpu.SemaphoreType.DMA((len(sources),)),
                pltpu.SemaphoreType.DMA((len(out_sizes),)),
            ],
        ),
        out_shape=[
            jax.ShapeDtypeStruct((size, tile, width), jnp.bfloat16)
            for size in out_sizes
        ],
        compiler_params=pltpu.CompilerParams(vmem_limit_bytes=VMEM_LIMIT),
        cost_estimate=pl.CostEstimate(
            flops=2 * slots * tile * tile * width,
            bytes_accessed=slots * tile * tile * 2,
            transcendentals=0,
        ),
    )(live, take, put, adjacency, *sources)


def split_dot(exact, other, dims):
    high = exact.astype(jnp.bfloat16)
    low = (exact - high.astype(jnp.float32)).astype(jnp.bfloat16)
    dot = functools.partial(
        lax.dot_general, dimension_numbers=dims, preferred_element_type=jnp.float32
    )
    return dot(high, other) + dot(low, other)


def middle_kernel(h0, h1, h2, h3, weight, bias, cotangent, out, grad, load):
    total = (
        h0[...].astype(jnp.float32)
        + h1[...].astype(jnp.float32)
        + h2[...].astype(jnp.float32)
        + h3[...].astype(jnp.float32)
    )
    shifted = split_dot(total, weight[...], (((1,), (0,)), ((), ()))) + bias[...]
    tanh_term = jnp.tanh(GELU_ROOT * (shifted + GELU_CUBIC * shifted * shifted * shifted))
    out[...] = (0.5 * shifted * (1.0 + tanh_term)).astype(jnp.bfloat16)
    slope = 0.5 * (1.0 + tanh_term) + 0.5 * shifted * (
        1.0 - tanh_term * tanh_term
    ) * GELU_ROOT * (1.0 + 3.0 * GELU_CUBIC * shifted * shifted)
    pre_grad = cotangent[...].astype(jnp.float32) * slope
    rounded = pre_grad.astype(jnp.bfloat16)
    grad[...] = rounded
    rows = (((0,), (0,)), ((), ()))
    load[:, : total.shape[1]] = split_dot(total, rounded, rows)
    ones = jnp.ones((total.shape[0], LANES), jnp.bfloat16)
    load[:, total.shape[1] :] = split_dot(pre_grad, ones, rows)


def middle(pieces, weight, bias, cotangent):
    rows, width = cotangent.shape
    vmem = pl.BlockSpec(memory_space=pltpu.VMEM)
    return pl.pallas_call(
        middle_kernel,
        in_specs=[vmem] * 7,
        out_specs=[vmem] * 3,
        out_shape=[
            jax.ShapeDtypeStruct((rows, width), jnp.bfloat16),
            jax.ShapeDtypeStruct((rows, width), jnp.bfloat16),
            jax.ShapeDtypeStruct((width, width + LANES), jnp.float32),
        ],
        compiler_params=pltpu.CompilerParams(vmem_limit_bytes=VMEM_LIMIT),
    )(*pieces, weight, bias.reshape(1, width), cotangent)


def last_kernel(pieces, weight, out):
    total = pieces[0].astype(jnp.float32)
    for k in range(1, pieces.shape[0]):
        total += pieces[k].astype(jnp.float32)
    out[...] = lax.dot_general(
        total.astype(jnp.bfloat16),
        weight[...],
        (((1,), (1,)), ((), ())),
        preferred_element_type=jnp.float32,
    ).astype(jnp.bfloat16)


def last(pieces, weight):
    _, rows, width = pieces.shape
    vmem = pl.BlockSpec(memory_space=pltpu.VMEM)
    return pl.pallas_call(
        last_kernel,
        in_specs=[vmem] * 2,
        out_specs=vmem,
        out_shape=jax.ShapeDtypeStruct((rows, width), jnp.bfloat16),
    )(pieces, weight)


def merge(pieces):
    return sum((p.astype(jnp.float32) for p in pieces[1:]), pieces[0].astype(jnp.float32)).astype(
        jnp.bfloat16
    )


def shards(features, cotangent, weight, bias, adjacency, tile_rows, tile_cols, live_tiles):
    vertices, width = features.shape
    tile = adjacency.shape[2]
    scale = 1.0 / math.sqrt(vertices * N_ROW * N_COL)
    live = live_tiles.reshape(1)
    row_id, col_id = lax.axis_index("row"), lax.axis_index("col")
    my_x, my_zl = row_id // N_ZL, row_id % N_ZL
    my_zh, my_y, my_core = col_id // 8, col_id // 2 % 4, col_id % 2

    per = vertices // tile
    r, c = tile_rows[0], tile_cols[0]
    rc, cc = r // per, c // per
    r_zh, r_y, r_core = rc // 8, rc // 2 % 4, rc % 2
    c_x, c_zl = cc // 2, cc % 2
    half = (r_core ^ my_core) * 16
    ahead = (r_zh - my_zh) & 3
    part = ((ahead == 3) | (ahead == 0)).astype(jnp.int32)
    place = ((ahead == 1) | (ahead == 0)).astype(jnp.int32)
    put_rows = (half + part * 8 + ((r_y - my_y) & 3) * 2 + place) * per + r % per
    take_rows = (half + ((my_y - r_y) & 3) * 4 + ((my_zh - r_zh) & 3)) * per + r % per
    take_cols = (((my_x - c_x) & 3) * 2 + (c_zl ^ my_zl)) * per + c % per

    moves = [(dx, dzl) for dx in range(N_X) for dzl in range(N_ZL)]
    with jax.named_scope("gather_features"):
        sources = [features] + [row_shift(features, *m) for m in moves[1:]]
    with jax.named_scope("tiles_forward"):
        parts = tile_sum(
            adjacency, live, take_cols, put_rows, sources, [8 * per] * 4, False
        )
    with jax.named_scope("sum_over_col"):
        sums = []
        for keep, send in zip(parts[:2], parts[2:]):
            other = col_shift(send, dcore=1)
            cut = [slice(2 * per * k, 2 * per * (k + 1)) for k in range(N_Y)]
            added = [merge([keep[s], other[s]]) for s in cut]
            arrived = [added[0]] + [col_shift(added[k], dy=k) for k in (2, 1, 3)]
            sums.append(merge([p[:per] for p in arrived]))
            sums.append(merge([p[per:] for p in arrived]))
        pieces = [sums[3]] + [col_shift(sums[i], dzh=k) for i, k in enumerate((2, 1, 3))]
        pieces = [p.reshape(vertices, width) for p in pieces]
    with jax.named_scope("pointwise"):
        layer_out, grad, load = middle(pieces, weight, bias, cotangent)
    with jax.named_scope("gather_gradients"):
        stack = jnp.concatenate([col_shift(grad, dzh=k) for k in range(1, N_ZH)])
        ours = [col_shift(grad, dy=k) for k in range(1, N_Y)]
    with jax.named_scope("sum_weight_grad"):
        load = lax.all_to_all(load[:, None], ("row", "col"), 0, 0, tiled=True)
        load, stack, *ours = lax.optimization_barrier((load, stack, *ours))
        total = jnp.sum(load, axis=0, keepdims=True) * scale
        spread = jnp.broadcast_to(total, load.shape)
        load = lax.all_to_all(spread, ("row", "col"), 0, 0, tiled=True)
    with jax.named_scope("gather_gradients"):
        theirs = [col_shift(stack, dy=k) for k in range(1, N_Y)]
        *theirs, load = lax.optimization_barrier((*theirs, load))
        here = [grad, stack]
        for pair in zip(ours, theirs):
            here += pair
        there = [col_shift(p, dcore=1) for p in here]
    weight_grad, bias_grad = load[:, 0, :width], load[:, 0, width]
    with jax.named_scope("tiles_backward"):
        (back,) = tile_sum(adjacency, live, take_rows, c, here + there, [N_ROW * per], True)
    with jax.named_scope("sum_over_row"):
        back = lax.all_to_all(
            back.reshape(N_ROW, vertices, width), "row", 0, 0, tiled=True
        )
        features_grad = last(back, weight)
    return layer_out, features_grad, weight_grad, bias_grad


def solution(mesh):
    placed = (
        P(("row", "col"), None),
        P(("row", "col"), None),
        P(),
        P(),
        P("row", "col", None, None),
        P("row", "col"),
        P("row", "col"),
        P("row", "col"),
    )
    return jax.shard_map(
        shards,
        mesh=mesh,
        in_specs=placed,
        out_specs=(P(("row", "col"), None), P(("row", "col"), None), P(), P()),
        check_vma=False,
    )
```

```python
import functools
import math

import jax
import jax.numpy as jnp
from jax import lax
from jax.experimental import pallas as pl
from jax.experimental.pallas import tpu as pltpu
from jax.sharding import PartitionSpec as P

GELU_ROOT = 0.7978845608028654
GELU_CUBIC = 0.044715

N_X, N_ZL, N_ZH, N_Y, N_CORE = 4, 2, 4, 4, 2
N_ROW = N_X * N_ZL
N_COL = N_ZH * N_Y * N_CORE
GROUP = 24
VMEM_LIMIT = 60 * 1024 * 1024
LANES = 128


def row_shift(value, dx, dzl):
    pairs = []
    for i in range(N_ROW):
        x, zl = divmod(i, N_ZL)
        pairs.append((i, (x + dx) % N_X * N_ZL + (zl ^ dzl)))
    return lax.ppermute(value, "row", pairs)


def col_shift(value, dzh=0, dy=0, dcore=0):
    pairs = []
    for i in range(N_COL):
        zh, y, core = i // (N_Y * N_CORE), i // N_CORE % N_Y, i % N_CORE
        pairs.append(
            (i, ((zh + dzh) % N_ZH * N_Y + (y + dy) % N_Y) * N_CORE + (core ^ dcore))
        )
    return lax.ppermute(value, "col", pairs)


def tile_kernel(transposed, src_sizes, out_sizes, live, take, put, tiles, *refs):
    n_src, n_out = len(src_sizes), len(out_sizes)
    sources = refs[:n_src]
    outs = refs[n_src : n_src + n_out]
    held, src, acc, staged, tile_sems, in_sems, out_sems = refs[n_src + n_out :]
    groups = live[0] // GROUP

    def tile_copy(g):
        rows = pl.ds(g * GROUP, GROUP)
        return pltpu.make_async_copy(tiles.at[0, rows], held.at[rows], tile_sems.at[g])

    copies, first = [], 0
    for k, size in enumerate(src_sizes):
        copies.append(
            pltpu.make_async_copy(sources[k], src.at[pl.ds(first, size)], in_sems.at[k])
        )
        first += size
    for copy in copies:
        copy.start()

    @pl.loop(0, groups)
    def _(g):
        tile_copy(g).start()

    @pl.loop(0, acc.shape[0])
    def _(i):
        acc[i] = jnp.zeros(acc.shape[1:], jnp.float32)

    for copy in copies:
        copy.wait()

    @pl.loop(0, groups)
    def _(g):
        tile_copy(g).wait()

        @pl.loop(0, GROUP // 8)
        def _(i):
            for j in range(8):
                slot = g * GROUP + i * 8 + j
                product = lax.dot_general(
                    held[slot],
                    src[take[slot]],
                    (((0 if transposed else 1,), (0,)), ((), ())),
                    preferred_element_type=jnp.float32,
                )
                acc[put[slot]] += product

    copies, first = [], 0
    for k, size in enumerate(out_sizes):
        start = first

        @pl.loop(0, size)
        def _(i):
            staged[start + i] = acc[start + i].astype(jnp.bfloat16)

        copies.append(
            pltpu.make_async_copy(staged.at[pl.ds(start, size)], outs[k], out_sems.at[k])
        )
        copies[-1].start()
        first += size
    for copy in copies:
        copy.wait()


def tile_sum(adjacency, live, take, put, sources, out_sizes, transposed):
    slots, tile = adjacency.shape[1], adjacency.shape[2]
    width = sources[0].shape[-1]
    sources = [s.reshape(-1, tile, width) for s in sources]
    src_sizes = [s.shape[0] for s in sources]
    anywhere = pl.BlockSpec(memory_space=pl.ANY)
    scalars = pl.BlockSpec(memory_space=pltpu.SMEM)
    return pl.pallas_call(
        functools.partial(tile_kernel, transposed, src_sizes, out_sizes),
        in_specs=[scalars] * 3 + [anywhere] * (1 + len(sources)),
        out_specs=[anywhere] * len(out_sizes),
        scratch_shapes=[
            pltpu.VMEM((slots, tile, tile), jnp.bfloat16),
            pltpu.VMEM((sum(src_sizes), tile, width), jnp.bfloat16),
            pltpu.VMEM((sum(out_sizes), tile, width), jnp.float32),
            pltpu.VMEM((sum(out_sizes), tile, width), jnp.bfloat16),
            pltpu.SemaphoreType.DMA((slots // GROUP,)),
            pltpu.SemaphoreType.DMA((len(sources),)),
            pltpu.SemaphoreType.DMA((len(out_sizes),)),
        ],
        out_shape=[
            jax.ShapeDtypeStruct((size, tile, width), jnp.bfloat16)
            for size in out_sizes
        ],
        compiler_params=pltpu.CompilerParams(vmem_limit_bytes=VMEM_LIMIT),
        cost_estimate=pl.CostEstimate(
            flops=2 * slots * tile * tile * width,
            bytes_accessed=slots * tile * tile * 2,
            transcendentals=0,
        ),
    )(live, take, put, adjacency, *sources)


def split_dot(exact, other, dims):
    high = exact.astype(jnp.bfloat16)
    low = (exact - high.astype(jnp.float32)).astype(jnp.bfloat16)
    dot = functools.partial(
        lax.dot_general, dimension_numbers=dims, preferred_element_type=jnp.float32
    )
    return dot(high, other) + dot(low, other)


def middle_kernel(h0, h1, h2, h3, weight, bias, cotangent, out, grad, total_out, pre_out):
    total = (
        h0[...].astype(jnp.float32)
        + h1[...].astype(jnp.float32)
        + h2[...].astype(jnp.float32)
        + h3[...].astype(jnp.float32)
    )
    shifted = split_dot(total, weight[...], (((1,), (0,)), ((), ()))) + bias[...]
    tanh_term = jnp.tanh(GELU_ROOT * (shifted + GELU_CUBIC * shifted * shifted * shifted))
    out[...] = (0.5 * shifted * (1.0 + tanh_term)).astype(jnp.bfloat16)
    slope = 0.5 * (1.0 + tanh_term) + 0.5 * shifted * (
        1.0 - tanh_term * tanh_term
    ) * GELU_ROOT * (1.0 + 3.0 * GELU_CUBIC * shifted * shifted)
    pre_grad = cotangent[...].astype(jnp.float32) * slope
    grad[...] = pre_grad.astype(jnp.bfloat16)
    total_out[...] = total
    pre_out[...] = pre_grad


def middle(pieces, weight, bias, cotangent):
    rows, width = cotangent.shape
    vmem = pl.BlockSpec(memory_space=pltpu.VMEM)
    return pl.pallas_call(
        middle_kernel,
        in_specs=[vmem] * 7,
        out_specs=[vmem] * 4,
        out_shape=[jax.ShapeDtypeStruct((rows, width), jnp.bfloat16)] * 2
        + [jax.ShapeDtypeStruct((rows, width), jnp.float32)] * 2,
        compiler_params=pltpu.CompilerParams(vmem_limit_bytes=VMEM_LIMIT),
    )(*pieces, weight, bias.reshape(1, width), cotangent)


def load_kernel(total, pre_grad, load):
    width = total.shape[1]
    rows = (((0,), (0,)), ((), ()))
    rounded = pre_grad[...].astype(jnp.bfloat16)
    load[:, :width] = split_dot(total[...], rounded, rows)
    ones = jnp.ones((total.shape[0], LANES), jnp.bfloat16)
    load[:, width:] = split_dot(pre_grad[...], ones, rows)


def loads(total, pre_grad):
    width = total.shape[1]
    vmem = pl.BlockSpec(memory_space=pltpu.VMEM)
    return pl.pallas_call(
        load_kernel,
        in_specs=[vmem] * 2,
        out_specs=vmem,
        out_shape=jax.ShapeDtypeStruct((width, width + LANES), jnp.float32),
        compiler_params=pltpu.CompilerParams(vmem_limit_bytes=VMEM_LIMIT),
    )(total, pre_grad)


def last_kernel(pieces, weight, out):
    total = pieces[0].astype(jnp.float32)
    for k in range(1, pieces.shape[0]):
        total += pieces[k].astype(jnp.float32)
    out[...] = lax.dot_general(
        total.astype(jnp.bfloat16),
        weight[...],
        (((1,), (1,)), ((), ())),
        preferred_element_type=jnp.float32,
    ).astype(jnp.bfloat16)


def last(pieces, weight):
    _, rows, width = pieces.shape
    vmem = pl.BlockSpec(memory_space=pltpu.VMEM)
    return pl.pallas_call(
        last_kernel,
        in_specs=[vmem] * 2,
        out_specs=vmem,
        out_shape=jax.ShapeDtypeStruct((rows, width), jnp.bfloat16),
    )(pieces, weight)


def merge(pieces):
    return sum((p.astype(jnp.float32) for p in pieces[1:]), pieces[0].astype(jnp.float32)).astype(
        jnp.bfloat16
    )


def shards(features, cotangent, weight, bias, adjacency, tile_rows, tile_cols, live_tiles):
    vertices, width = features.shape
    tile = adjacency.shape[2]
    scale = 1.0 / math.sqrt(vertices * N_ROW * N_COL)
    live = live_tiles.reshape(1)
    row_id, col_id = lax.axis_index("row"), lax.axis_index("col")
    my_x, my_zl = row_id // N_ZL, row_id % N_ZL
    my_zh, my_y, my_core = col_id // 8, col_id // 2 % 4, col_id % 2

    per = vertices // tile
    r, c = tile_rows[0], tile_cols[0]
    rc, cc = r // per, c // per
    r_zh, r_y, r_core = rc // 8, rc // 2 % 4, rc % 2
    c_x, c_zl = cc // 2, cc % 2
    half = (r_core ^ my_core) * 16
    ahead = (r_zh - my_zh) & 3
    part = ((ahead == 3) | (ahead == 0)).astype(jnp.int32)
    place = ((ahead == 1) | (ahead == 0)).astype(jnp.int32)
    put_rows = (half + part * 8 + ((r_y - my_y) & 3) * 2 + place) * per + r % per
    back_y, back_zh = (my_y - r_y) & 3, (my_zh - r_zh) & 3
    take_rows = jnp.where(back_zh == 0, 3 + back_y, 3 * back_y + 3 + back_zh)
    take_rows = jnp.where(back_y == 0, back_zh, take_rows)
    take_rows = (half + take_rows) * per + r % per
    take_cols = (((my_x - c_x) & 3) * 2 + (c_zl ^ my_zl)) * per + c % per

    moves = [(dx, dzl) for dx in range(N_X) for dzl in range(N_ZL)]
    with jax.named_scope("gather_features"):
        sources = [features] + [row_shift(features, *m) for m in moves[1:]]
    with jax.named_scope("tiles_forward"):
        parts = tile_sum(
            adjacency, live, take_cols, put_rows, sources, [8 * per] * 4, False
        )
    with jax.named_scope("sum_over_col"):
        sums, pieces = [], []
        for keep, send in zip(parts[:2], parts[2:]):
            other = col_shift(send, dcore=1)
            cut = [slice(2 * per * k, 2 * per * (k + 1)) for k in range(N_Y)]
            added = [merge([keep[s], other[s]]) for s in cut]
            arrived = [added[0]] + [col_shift(added[k], dy=k) for k in (2, 1, 3)]
            if pieces:
                *arrived, pieces[1] = lax.optimization_barrier((*arrived, pieces[1]))
            sums = [merge([p[:per] for p in arrived]), merge([p[per:] for p in arrived])]
            if not pieces:
                pieces = [col_shift(sums[0], dzh=2), col_shift(sums[1], dzh=1)]
            else:
                pieces += [col_shift(sums[0], dzh=3), sums[1]]
        pieces = [p.reshape(vertices, width) for p in pieces]
    with jax.named_scope("pointwise"):
        layer_out, grad, total, pre_grad = middle(pieces, weight, bias, cotangent)
    with jax.named_scope("gather_gradients"):
        near = [col_shift(grad, dzh=k) for k in range(1, N_ZH)]
        ours = jnp.concatenate([col_shift(grad, dy=k) for k in range(1, N_Y)])
        stack = jnp.concatenate(near)
    with jax.named_scope("sum_weight_grad"):
        load = loads(total, pre_grad).reshape(N_COL, -1, width + LANES)
        load = jnp.sum(lax.all_to_all(load, "col", 0, 0, tiled=True), axis=0)
        load = jnp.broadcast_to(load, (N_ROW,) + load.shape)
        load = jnp.sum(lax.all_to_all(load, "row", 0, 0, tiled=True), axis=0) * scale
        load = jnp.broadcast_to(load, (N_COL,) + load.shape)
        load = lax.all_to_all(load, "col", 0, 0, tiled=True).reshape(width, -1)
        weight_grad, bias_grad = load[:, :width], load[:, width]
    with jax.named_scope("gather_gradients"):
        theirs = [col_shift(stack, dy=k) for k in range(1, N_Y)]
        here = [grad, stack, ours] + theirs
        there = [col_shift(p, dcore=1) for p in here]
    with jax.named_scope("tiles_backward"):
        (back,) = tile_sum(adjacency, live, take_rows, c, here + there, [N_ROW * per], True)
    with jax.named_scope("sum_over_row"):
        back = lax.all_to_all(
            back.reshape(N_ROW, vertices, width), "row", 0, 0, tiled=True
        )
        features_grad = last(back, weight)
    return layer_out, features_grad, weight_grad, bias_grad


def solution(mesh):
    placed = (
        P(("row", "col"), None),
        P(("row", "col"), None),
        P(),
        P(),
        P("row", "col", None, None),
        P("row", "col"),
        P("row", "col"),
        P("row", "col"),
    )
    return jax.shard_map(
        shards,
        mesh=mesh,
        in_specs=placed,
        out_specs=(P(("row", "col"), None), P(("row", "col"), None), P(), P()),
        check_vma=False,
    )
```

```python
import functools
import math

import jax
import jax.numpy as jnp
from jax import lax
from jax.experimental import pallas as pl
from jax.experimental.pallas import tpu as pltpu
from jax.sharding import PartitionSpec as P

GELU_ROOT = 0.7978845608028654
GELU_CUBIC = 0.044715

N_X, N_ZL, N_ZH, N_Y, N_CORE = 4, 2, 4, 4, 2
N_ROW = N_X * N_ZL
N_COL = N_ZH * N_Y * N_CORE
GROUP = 24
VMEM_LIMIT = 60 * 1024 * 1024
LANES = 128


def col_shift(value, dzh=0, dy=0, dcore=0):
    pairs = []
    for i in range(N_COL):
        zh, y, core = i // (N_Y * N_CORE), i // N_CORE % N_Y, i % N_CORE
        pairs.append(
            (i, ((zh + dzh) % N_ZH * N_Y + (y + dy) % N_Y) * N_CORE + (core ^ dcore))
        )
    return lax.ppermute(value, "col", pairs)


def tile_kernel(transposed, src_sizes, out_sizes, live, take, put, tiles, *refs):
    n_src, n_out = len(src_sizes), len(out_sizes)
    sources = refs[:n_src]
    outs = refs[n_src : n_src + n_out]
    held, src, acc, staged, tile_sems, in_sems, out_sems = refs[n_src + n_out :]
    groups = live[0] // GROUP

    def tile_copy(g):
        rows = pl.ds(g * GROUP, GROUP)
        return pltpu.make_async_copy(tiles.at[0, rows], held.at[rows], tile_sems.at[g])

    copies, first = [], 0
    for k, size in enumerate(src_sizes):
        copies.append(
            pltpu.make_async_copy(sources[k], src.at[pl.ds(first, size)], in_sems.at[k])
        )
        first += size
    for copy in copies:
        copy.start()

    @pl.loop(0, groups)
    def _(g):
        tile_copy(g).start()

    @pl.loop(0, acc.shape[0])
    def _(i):
        acc[i] = jnp.zeros(acc.shape[1:], jnp.float32)

    for copy in copies:
        copy.wait()

    @pl.loop(0, groups)
    def _(g):
        tile_copy(g).wait()

        for j in range(GROUP):
            slot = g * GROUP + j
            product = lax.dot_general(
                held[slot],
                src[take[slot]],
                (((0 if transposed else 1,), (0,)), ((), ())),
                preferred_element_type=jnp.float32,
            )
            acc[put[slot]] += product

    copies, first = [], 0
    for k, size in enumerate(out_sizes):
        start = first

        @pl.loop(0, size)
        def _(i):
            staged[start + i] = acc[start + i].astype(jnp.bfloat16)

        copies.append(
            pltpu.make_async_copy(staged.at[pl.ds(start, size)], outs[k], out_sems.at[k])
        )
        copies[-1].start()
        first += size
    for copy in copies:
        copy.wait()


def tile_sum(adjacency, live, take, put, sources, out_sizes, transposed):
    slots, tile = adjacency.shape[1], adjacency.shape[2]
    width = sources[0].shape[-1]
    sources = [s.reshape(-1, tile, width) for s in sources]
    src_sizes = [s.shape[0] for s in sources]
    anywhere = pl.BlockSpec(memory_space=pl.ANY)
    scalars = pl.BlockSpec(memory_space=pltpu.SMEM)
    return pl.pallas_call(
        functools.partial(tile_kernel, transposed, src_sizes, out_sizes),
        in_specs=[scalars] * 3 + [anywhere] * (1 + len(sources)),
        out_specs=[anywhere] * len(out_sizes),
        scratch_shapes=[
            pltpu.VMEM((slots, tile, tile), jnp.bfloat16),
            pltpu.VMEM((sum(src_sizes), tile, width), jnp.bfloat16),
            pltpu.VMEM((sum(out_sizes), tile, width), jnp.float32),
            pltpu.VMEM((sum(out_sizes), tile, width), jnp.bfloat16),
            pltpu.SemaphoreType.DMA((slots // GROUP,)),
            pltpu.SemaphoreType.DMA((len(sources),)),
            pltpu.SemaphoreType.DMA((len(out_sizes),)),
        ],
        out_shape=[
            jax.ShapeDtypeStruct((size, tile, width), jnp.bfloat16)
            for size in out_sizes
        ],
        compiler_params=pltpu.CompilerParams(vmem_limit_bytes=VMEM_LIMIT),
        cost_estimate=pl.CostEstimate(
            flops=2 * slots * tile * tile * width,
            bytes_accessed=slots * tile * tile * 2,
            transcendentals=0,
        ),
    )(live, take, put, adjacency, *sources)


def split_dot(exact, other, dims):
    high = exact.astype(jnp.bfloat16)
    low = (exact - high.astype(jnp.float32)).astype(jnp.bfloat16)
    dot = functools.partial(
        lax.dot_general, dimension_numbers=dims, preferred_element_type=jnp.float32
    )
    return dot(high, other) + dot(low, other)


def middle_kernel(h0, h1, h2, h3, weight, bias, cotangent, out, grad, total_out, pre_out):
    total = (
        h0[...].astype(jnp.float32)
        + h1[...].astype(jnp.float32)
        + h2[...].astype(jnp.float32)
        + h3[...].astype(jnp.float32)
    )
    shifted = split_dot(total, weight[...], (((1,), (0,)), ((), ()))) + bias[...]
    tanh_term = jnp.tanh(GELU_ROOT * (shifted + GELU_CUBIC * shifted * shifted * shifted))
    out[...] = (0.5 * shifted * (1.0 + tanh_term)).astype(jnp.bfloat16)
    slope = 0.5 * (1.0 + tanh_term) + 0.5 * shifted * (
        1.0 - tanh_term * tanh_term
    ) * GELU_ROOT * (1.0 + 3.0 * GELU_CUBIC * shifted * shifted)
    pre_grad = cotangent[...].astype(jnp.float32) * slope
    grad[...] = pre_grad.astype(jnp.bfloat16)
    total_out[...] = total
    pre_out[...] = pre_grad


def middle(pieces, weight, bias, cotangent):
    rows, width = cotangent.shape
    vmem = pl.BlockSpec(memory_space=pltpu.VMEM)
    return pl.pallas_call(
        middle_kernel,
        in_specs=[vmem] * 7,
        out_specs=[vmem] * 4,
        out_shape=[jax.ShapeDtypeStruct((rows, width), jnp.bfloat16)] * 2
        + [jax.ShapeDtypeStruct((rows, width), jnp.float32)] * 2,
        compiler_params=pltpu.CompilerParams(vmem_limit_bytes=VMEM_LIMIT),
    )(*pieces, weight, bias.reshape(1, width), cotangent)


def load_kernel(total, pre_grad, load):
    width = total.shape[1]
    rows = (((0,), (0,)), ((), ()))
    rounded = pre_grad[...].astype(jnp.bfloat16)
    load[:, :width] = split_dot(total[...], rounded, rows)
    ones = jnp.ones((total.shape[0], LANES), jnp.bfloat16)
    load[:, width:] = split_dot(pre_grad[...], ones, rows)


def loads(total, pre_grad):
    width = total.shape[1]
    vmem = pl.BlockSpec(memory_space=pltpu.VMEM)
    return pl.pallas_call(
        load_kernel,
        in_specs=[vmem] * 2,
        out_specs=vmem,
        out_shape=jax.ShapeDtypeStruct((width, width + LANES), jnp.float32),
        compiler_params=pltpu.CompilerParams(vmem_limit_bytes=VMEM_LIMIT),
    )(total, pre_grad)


def last_kernel(pieces, weight, out):
    total = pieces[0].astype(jnp.float32)
    for k in range(1, pieces.shape[0]):
        total += pieces[k].astype(jnp.float32)
    out[...] = lax.dot_general(
        total.astype(jnp.bfloat16),
        weight[...],
        (((1,), (1,)), ((), ())),
        preferred_element_type=jnp.float32,
    ).astype(jnp.bfloat16)


def last(pieces, weight):
    _, rows, width = pieces.shape
    vmem = pl.BlockSpec(memory_space=pltpu.VMEM)
    return pl.pallas_call(
        last_kernel,
        in_specs=[vmem] * 2,
        out_specs=vmem,
        out_shape=jax.ShapeDtypeStruct((rows, width), jnp.bfloat16),
        compiler_params=pltpu.CompilerParams(vmem_limit_bytes=VMEM_LIMIT),
    )(pieces, weight)


def merge(pieces):
    return sum((p.astype(jnp.float32) for p in pieces[1:]), pieces[0].astype(jnp.float32)).astype(
        jnp.bfloat16
    )


def shards(features, cotangent, weight, bias, adjacency, tile_rows, tile_cols, live_tiles):
    vertices, width = features.shape
    tile = adjacency.shape[2]
    scale = 1.0 / math.sqrt(vertices * N_ROW * N_COL)
    live = live_tiles.reshape(1)
    col_id = lax.axis_index("col")
    my_zh, my_y, my_core = col_id // 8, col_id // 2 % 4, col_id % 2

    per = vertices // tile
    r, c = tile_rows[0], tile_cols[0]
    rc = r // per
    r_zh, r_y, r_core = rc // 8, rc // 2 % 4, rc % 2
    half = (r_core ^ my_core) * 16
    ahead = (r_zh - my_zh) & 3
    part = ((ahead == 3) | (ahead == 0)).astype(jnp.int32)
    place = ((ahead == 1) | (ahead == 0)).astype(jnp.int32)
    put_rows = (half + part * 8 + ((r_y - my_y) & 3) * 2 + place) * per + r % per
    take_rows = (half + ((my_y - r_y) & 3) * 4 + ((my_zh - r_zh) & 3)) * per + r % per

    with jax.named_scope("gather_features"):
        copies = jnp.broadcast_to(features, (N_ROW,) + features.shape)
        source = lax.all_to_all(copies, "row", 0, 0, tiled=True)
    with jax.named_scope("tiles_forward"):
        parts = tile_sum(
            adjacency, live, c, put_rows, [source], [8 * per] * 4, False
        )
    with jax.named_scope("sum_over_col"):
        sums, pieces = [], []
        for keep, send in zip(parts[:2], parts[2:]):
            other = col_shift(send, dcore=1)
            cut = [slice(2 * per * k, 2 * per * (k + 1)) for k in range(N_Y)]
            added = [merge([keep[s], other[s]]) for s in cut]
            arrived = [added[0]] + [col_shift(added[k], dy=k) for k in (2, 1, 3)]
            if pieces:
                *arrived, pieces[1] = lax.optimization_barrier((*arrived, pieces[1]))
            sums = [merge([p[:per] for p in arrived]), merge([p[per:] for p in arrived])]
            if not pieces:
                pieces = [col_shift(sums[0], dzh=2), col_shift(sums[1], dzh=1)]
            else:
                pieces += [col_shift(sums[0], dzh=3), sums[1]]
        pieces = [p.reshape(vertices, width) for p in pieces]
    with jax.named_scope("pointwise"):
        layer_out, grad, total, pre_grad = middle(pieces, weight, bias, cotangent)
    with jax.named_scope("gather_gradients"):
        near = [col_shift(grad, dzh=k) for k in range(1, N_ZH)]
        load = loads(total, pre_grad).reshape(N_COL, -1, width + LANES)
        *near, load = lax.optimization_barrier((*near, load))
        here = [jnp.concatenate([grad] + near)]
    with jax.named_scope("sum_weight_grad"):
        load = jnp.sum(lax.all_to_all(load, "col", 0, 0, tiled=True), axis=0)
        load = jnp.broadcast_to(load, (N_ROW,) + load.shape)
        load = jnp.sum(lax.all_to_all(load, "row", 0, 0, tiled=True), axis=0) * scale
        load = jnp.broadcast_to(load, (N_COL,) + load.shape)
        load = lax.all_to_all(load, "col", 0, 0, tiled=True).reshape(width, -1)
        weight_grad, bias_grad = load[:, :width], load[:, width]
    with jax.named_scope("gather_gradients"):
        here += [col_shift(here[0], dy=k) for k in range(1, N_Y)]
        there = [col_shift(p, dcore=1) for p in here]
    with jax.named_scope("tiles_backward"):
        (back,) = tile_sum(adjacency, live, take_rows, c, here + there, [N_ROW * per], True)
    with jax.named_scope("sum_over_row"):
        back = lax.all_to_all(
            back.reshape(N_ROW, vertices, width), "row", 0, 0, tiled=True
        )
        features_grad = last(back, weight)
    return layer_out, features_grad, weight_grad, bias_grad


def solution(mesh):
    placed = (
        P(("row", "col"), None),
        P(("row", "col"), None),
        P(),
        P(),
        P("row", "col", None, None),
        P("row", "col"),
        P("row", "col"),
        P("row", "col"),
    )
    return jax.shard_map(
        shards,
        mesh=mesh,
        in_specs=placed,
        out_specs=(P(("row", "col"), None), P(("row", "col"), None), P(), P()),
        check_vma=False,
    )
```

```python
import functools
import math

import jax
import jax.numpy as jnp
from jax import lax
from jax.experimental import pallas as pl
from jax.experimental.pallas import tpu as pltpu
from jax.sharding import PartitionSpec as P

GELU_ROOT = 0.7978845608028654
GELU_CUBIC = 0.044715

N_X, N_ZL, N_ZH, N_Y, N_CORE = 4, 2, 4, 4, 2
N_ROW = N_X * N_ZL
N_COL = N_ZH * N_Y * N_CORE
GROUP = 24
VMEM_LIMIT = 60 * 1024 * 1024
LANES = 128


def row_shift(value, dx, dzl):
    pairs = []
    for i in range(N_ROW):
        x, zl = divmod(i, N_ZL)
        pairs.append((i, (x + dx) % N_X * N_ZL + (zl ^ dzl)))
    return lax.ppermute(value, "row", pairs)


def col_shift(value, dzh=0, dy=0, dcore=0):
    pairs = []
    for i in range(N_COL):
        zh, y, core = i // (N_Y * N_CORE), i // N_CORE % N_Y, i % N_CORE
        pairs.append(
            (i, ((zh + dzh) % N_ZH * N_Y + (y + dy) % N_Y) * N_CORE + (core ^ dcore))
        )
    return lax.ppermute(value, "col", pairs)


def tile_kernel(transposed, src_sizes, out_sizes, live, take, put, tiles, *refs):
    n_src, n_out = len(src_sizes), len(out_sizes)
    sources = refs[:n_src]
    outs = refs[n_src : n_src + n_out]
    held, src, acc, staged, tile_sems, in_sems, out_sems = refs[n_src + n_out :]
    groups = live[0] // GROUP

    def tile_copy(g):
        rows = pl.ds(g * GROUP, GROUP)
        return pltpu.make_async_copy(tiles.at[0, rows], held.at[rows], tile_sems.at[g])

    copies, first = [], 0
    for k, size in enumerate(src_sizes):
        copies.append(
            pltpu.make_async_copy(sources[k], src.at[pl.ds(first, size)], in_sems.at[k])
        )
        first += size
    for copy in copies:
        copy.start()

    @pl.loop(0, groups)
    def _(g):
        tile_copy(g).start()

    @pl.loop(0, acc.shape[0])
    def _(i):
        acc[i] = jnp.zeros(acc.shape[1:], jnp.float32)

    for copy in copies:
        copy.wait()

    @pl.loop(0, groups)
    def _(g):
        tile_copy(g).wait()

        for j in range(GROUP):
            slot = g * GROUP + j
            product = lax.dot_general(
                held[slot],
                src[take[slot]],
                (((0 if transposed else 1,), (0,)), ((), ())),
                preferred_element_type=jnp.float32,
            )
            acc[put[slot]] += product

    copies, first = [], 0
    for k, size in enumerate(out_sizes):
        start = first

        @pl.loop(0, size)
        def _(i):
            staged[start + i] = acc[start + i].astype(jnp.bfloat16)

        copies.append(
            pltpu.make_async_copy(staged.at[pl.ds(start, size)], outs[k], out_sems.at[k])
        )
        copies[-1].start()
        first += size
    for copy in copies:
        copy.wait()


def tile_sum(adjacency, live, take, put, sources, out_sizes, transposed):
    slots, tile = adjacency.shape[1], adjacency.shape[2]
    width = sources[0].shape[-1]
    sources = [s.reshape(-1, tile, width) for s in sources]
    src_sizes = [s.shape[0] for s in sources]
    anywhere = pl.BlockSpec(memory_space=pltpu.HBM)
    scalars = pl.BlockSpec(memory_space=pltpu.SMEM)
    return pl.pallas_call(
        functools.partial(tile_kernel, transposed, src_sizes, out_sizes),
        in_specs=[scalars] * 3 + [anywhere] * (1 + len(sources)),
        out_specs=[anywhere] * len(out_sizes),
        scratch_shapes=[
            pltpu.VMEM((slots, tile, tile), jnp.bfloat16),
            pltpu.VMEM((sum(src_sizes), tile, width), jnp.bfloat16),
            pltpu.VMEM((sum(out_sizes), tile, width), jnp.float32),
            pltpu.VMEM((sum(out_sizes), tile, width), jnp.bfloat16),
            pltpu.SemaphoreType.DMA((slots // GROUP,)),
            pltpu.SemaphoreType.DMA((len(sources),)),
            pltpu.SemaphoreType.DMA((len(out_sizes),)),
        ],
        out_shape=[
            jax.ShapeDtypeStruct((size, tile, width), jnp.bfloat16)
            for size in out_sizes
        ],
        compiler_params=pltpu.CompilerParams(vmem_limit_bytes=VMEM_LIMIT),
        cost_estimate=pl.CostEstimate(
            flops=2 * slots * tile * tile * width,
            bytes_accessed=slots * tile * tile * 2,
            transcendentals=0,
        ),
    )(live, take, put, adjacency, *sources)


def split_dot(exact, other, dims):
    high = exact.astype(jnp.bfloat16)
    low = (exact - high.astype(jnp.float32)).astype(jnp.bfloat16)
    dot = functools.partial(
        lax.dot_general, dimension_numbers=dims, preferred_element_type=jnp.float32
    )
    return dot(high, other) + dot(low, other)


def middle_kernel(count, *refs):
    weight, bias, cotangent, out, grad, total_out, pre_out = refs[count:]
    total = refs[0][...].astype(jnp.float32)
    for piece in refs[1:count]:
        total += piece[...].astype(jnp.float32)
    shifted = split_dot(total, weight[...], (((1,), (0,)), ((), ()))) + bias[...]
    tanh_term = jnp.tanh(GELU_ROOT * (shifted + GELU_CUBIC * shifted * shifted * shifted))
    out[...] = (0.5 * shifted * (1.0 + tanh_term)).astype(jnp.bfloat16)
    slope = 0.5 * (1.0 + tanh_term) + 0.5 * shifted * (
        1.0 - tanh_term * tanh_term
    ) * GELU_ROOT * (1.0 + 3.0 * GELU_CUBIC * shifted * shifted)
    pre_grad = cotangent[...].astype(jnp.float32) * slope
    grad[...] = pre_grad.astype(jnp.bfloat16)
    total_out[...] = total
    pre_out[...] = pre_grad


def middle(pieces, weight, bias, cotangent):
    rows, width = cotangent.shape
    vmem = pl.BlockSpec(memory_space=pltpu.VMEM)
    return pl.pallas_call(
        functools.partial(middle_kernel, len(pieces)),
        in_specs=[vmem] * (len(pieces) + 3),
        out_specs=[vmem] * 4,
        out_shape=[jax.ShapeDtypeStruct((rows, width), jnp.bfloat16)] * 2
        + [jax.ShapeDtypeStruct((rows, width), jnp.float32)] * 2,
        compiler_params=pltpu.CompilerParams(vmem_limit_bytes=VMEM_LIMIT),
    )(*pieces, weight, bias.reshape(1, width), cotangent)


def load_kernel(total, pre_grad, load):
    width = total.shape[1]
    rows = (((0,), (0,)), ((), ()))
    rounded = pre_grad[...].astype(jnp.bfloat16)
    load[:, :width] = split_dot(total[...], rounded, rows)
    ones = jnp.ones((total.shape[0], LANES), jnp.bfloat16)
    load[:, width:] = split_dot(pre_grad[...], ones, rows)


def loads(total, pre_grad):
    width = total.shape[1]
    vmem = pl.BlockSpec(memory_space=pltpu.VMEM)
    return pl.pallas_call(
        load_kernel,
        in_specs=[vmem] * 2,
        out_specs=vmem,
        out_shape=jax.ShapeDtypeStruct((width, width + LANES), jnp.float32),
        compiler_params=pltpu.CompilerParams(vmem_limit_bytes=VMEM_LIMIT),
    )(total, pre_grad)


def last_kernel(pieces, weight, out):
    total = pieces[0].astype(jnp.float32)
    for k in range(1, pieces.shape[0]):
        total += pieces[k].astype(jnp.float32)
    out[...] = lax.dot_general(
        total.astype(jnp.bfloat16),
        weight[...],
        (((1,), (1,)), ((), ())),
        preferred_element_type=jnp.float32,
    ).astype(jnp.bfloat16)


def last(pieces, weight):
    _, rows, width = pieces.shape
    vmem = pl.BlockSpec(memory_space=pltpu.VMEM)
    return pl.pallas_call(
        last_kernel,
        in_specs=[vmem] * 2,
        out_specs=vmem,
        out_shape=jax.ShapeDtypeStruct((rows, width), jnp.bfloat16),
        compiler_params=pltpu.CompilerParams(vmem_limit_bytes=VMEM_LIMIT),
    )(pieces, weight)


def spread_kernel(place, here, there, weight_grad, bias_grad):
    width = weight_grad.shape[1]
    chunk = weight_grad.shape[0] // N_COL
    for core, rows in enumerate((here, there)):
        for k in range(N_ZH * N_Y):
            y, zh = divmod(k, N_ZH)
            owner = (
                ((place[0] + N_ZH - zh) % N_ZH * N_Y + (place[1] + N_Y - y) % N_Y) * N_CORE
                + (place[2] + core) % N_CORE
            )
            put = pl.ds(pl.multiple_of(owner * chunk, chunk), chunk)
            weight_grad[put, :] = rows[chunk * k : chunk * (k + 1), :width]
            bias_grad[put, :] = rows[chunk * k : chunk * (k + 1), width:]


def spread(place, here, there, width):
    rows = here.shape[0] * N_CORE
    vmem = pl.BlockSpec(memory_space=pltpu.VMEM)
    return pl.pallas_call(
        spread_kernel,
        in_specs=[pl.BlockSpec(memory_space=pltpu.SMEM)] + [vmem] * 2,
        out_specs=[vmem] * 2,
        out_shape=[
            jax.ShapeDtypeStruct((rows, width), jnp.float32),
            jax.ShapeDtypeStruct((rows, here.shape[1] - width), jnp.float32),
        ],
    )(place, here, there)


def merge(pieces):
    return sum((p.astype(jnp.float32) for p in pieces[1:]), pieces[0].astype(jnp.float32)).astype(
        jnp.bfloat16
    )


def shards(features, cotangent, weight, bias, adjacency, tile_rows, tile_cols, live_tiles):
    vertices, width = features.shape
    tile = adjacency.shape[2]
    scale = 1.0 / math.sqrt(vertices * N_ROW * N_COL)
    live = live_tiles.reshape(1)
    row_id, col_id = lax.axis_index("row"), lax.axis_index("col")
    my_x, my_zl = row_id // N_ZL, row_id % N_ZL
    my_zh, my_y, my_core = col_id // 8, col_id // 2 % 4, col_id % 2

    per = vertices // tile
    r, c = tile_rows[0], tile_cols[0]
    rc, cc = r // per, c // per
    c_x, c_zl = cc // 2, cc % 2
    r_zh, r_y, r_core = rc // 8, rc // 2 % 4, rc % 2
    half = (r_core ^ my_core) * 16
    ahead = (r_zh - my_zh) & 3
    part = ((ahead == 3) | (ahead == 0)).astype(jnp.int32)
    place = ((ahead == 1) | (ahead == 0)).astype(jnp.int32)
    put_rows = (half + part * 8 + ((r_y - my_y) & 3) * 2 + place) * per + r % per
    take_cols = (((my_x - c_x) & 3) * 2 + (c_zl ^ my_zl)) * per + c % per
    take_rows = (half + ((my_y - r_y) & 3) * 4 + ((my_zh - r_zh) & 3)) * per + r % per

    moves = [(dx, dzl) for dx in range(N_X) for dzl in range(N_ZL)]
    with jax.named_scope("gather_features"):
        sources = [features] + [row_shift(features, *m) for m in moves[1:]]
    with jax.named_scope("tiles_forward"):
        parts = tile_sum(
            adjacency, live, take_cols, put_rows, sources, [8 * per] * 4, False
        )
    with jax.named_scope("sum_over_col"):
        others = [col_shift(send, dcore=1) for send in parts[2:]]

        def over_y(part, first, size):
            added = []
            for k in range(N_Y):
                rows = slice(2 * per * k + first * per, 2 * per * k + (first + size) * per)
                added.append(merge([parts[part][rows], others[part][rows]]))
            return [added[0]] + [col_shift(added[k], dy=k) for k in (2, 1, 3)]

        both = over_y(0, 0, 2)
        far = col_shift(merge([p[:per] for p in both]), dzh=2)
        near = col_shift(merge([p[per:] for p in both]), dzh=1)
        back = over_y(1, 0, 1)
        *back, near = lax.optimization_barrier((*back, near))
        pieces = over_y(1, 1, 1) + [far, near, col_shift(merge(back), dzh=3)]
        pieces = [p.reshape(vertices, width) for p in pieces]
    with jax.named_scope("pointwise"):
        layer_out, grad, total, pre_grad = middle(pieces, weight, bias, cotangent)
    with jax.named_scope("gather_gradients"):
        near = [col_shift(grad, dzh=k) for k in range(1, N_ZH)]
        load = loads(total, pre_grad).reshape(N_COL, -1, width + LANES)
        *near, load = lax.optimization_barrier((*near, load))
        here = [jnp.concatenate([grad] + near)]
    with jax.named_scope("sum_weight_grad"):
        load = jnp.sum(lax.all_to_all(load, "col", 0, 0, tiled=True), axis=0)
        load = jnp.broadcast_to(load, (N_ROW,) + load.shape)
        load = jnp.sum(lax.all_to_all(load, "row", 0, 0, tiled=True), axis=0) * scale
    with jax.named_scope("gather_gradients"):
        here += [col_shift(here[0], dy=k) for k in range(1, N_Y)]
        there = [col_shift(p, dcore=1) for p in here]
    with jax.named_scope("tiles_backward"):
        (back,) = tile_sum(adjacency, live, take_rows, c, here + there, [N_ROW * per], True)
    with jax.named_scope("sum_over_row"):
        back = back.reshape(N_ROW, vertices, width)
        back = lax.all_to_all(back, "row", 0, 0, tiled=True)
        features_grad = last(back, weight)
    with jax.named_scope("sum_weight_grad"):
        load = jnp.concatenate([load] + [col_shift(load, dzh=k) for k in range(1, N_ZH)])
        load = jnp.concatenate([load] + [col_shift(load, dy=k) for k in range(1, N_Y)])
        place = jnp.stack([my_zh, my_y, my_core]).astype(jnp.int32)
        weight_grad, bias_grad = spread(place, load, col_shift(load, dcore=1), width)
    return layer_out, features_grad, weight_grad, bias_grad[:, 0]


def solution(mesh):
    placed = (
        P(("row", "col"), None),
        P(("row", "col"), None),
        P(),
        P(),
        P("row", "col", None, None),
        P("row", "col"),
        P("row", "col"),
        P("row", "col"),
    )
    return jax.shard_map(
        shards,
        mesh=mesh,
        in_specs=placed,
        out_specs=(P(("row", "col"), None), P(("row", "col"), None), P(), P()),
        check_vma=False,
    )
```

```python
import functools
import math

import jax
import jax.numpy as jnp
from jax import lax
from jax.experimental import pallas as pl
from jax.experimental.pallas import tpu as pltpu
from jax.sharding import PartitionSpec as P

GELU_ROOT = 0.7978845608028654
GELU_CUBIC = 0.044715

N_X, N_ZL, N_ZH, N_Y, N_CORE = 4, 2, 4, 4, 2
N_ROW = N_X * N_ZL
N_COL = N_ZH * N_Y * N_CORE
GROUP = 24
VMEM_LIMIT = 65408 * 1024
LANES = 128


def row_shift(value, dx, dzl):
    pairs = []
    for i in range(N_ROW):
        x, zl = divmod(i, N_ZL)
        pairs.append((i, (x + dx) % N_X * N_ZL + (zl ^ dzl)))
    return lax.ppermute(value, "row", pairs)


def col_shift(value, dzh=0, dy=0, dcore=0):
    pairs = []
    for i in range(N_COL):
        zh, y, core = i // (N_Y * N_CORE), i // N_CORE % N_Y, i % N_CORE
        pairs.append(
            (i, ((zh + dzh) % N_ZH * N_Y + (y + dy) % N_Y) * N_CORE + (core ^ dcore))
        )
    return lax.ppermute(value, "col", pairs)


def tile_kernel(transposed, src_sizes, out_sizes, live, take, put, tiles, *refs):
    n_src, n_out = len(src_sizes), len(out_sizes)
    sources = refs[:n_src]
    outs = refs[n_src : n_src + n_out]
    held, src, acc, staged, tile_sems, in_sems, out_sems = refs[n_src + n_out :]
    groups = live[0] // GROUP

    def tile_copy(g):
        rows = pl.ds(g * GROUP, GROUP)
        return pltpu.make_async_copy(tiles.at[0, rows], held.at[rows], tile_sems.at[g])

    copies, first = [], 0
    for k, size in enumerate(src_sizes):
        copies.append(
            pltpu.make_async_copy(sources[k], src.at[pl.ds(first, size)], in_sems.at[k])
        )
        first += size
    for copy in copies:
        copy.start()

    @pl.loop(0, groups)
    def _(g):
        tile_copy(g).start()

    @pl.loop(0, acc.shape[0])
    def _(i):
        acc[i] = jnp.zeros(acc.shape[1:], jnp.float32)

    for copy in copies:
        copy.wait()

    @pl.loop(0, groups)
    def _(g):
        tile_copy(g).wait()

        for j in range(GROUP):
            slot = g * GROUP + j
            product = lax.dot_general(
                held[slot],
                src[take[slot]],
                (((0 if transposed else 1,), (0,)), ((), ())),
                preferred_element_type=jnp.float32,
            )
            acc[put[slot]] += product

    copies, first = [], 0
    for k, size in enumerate(out_sizes):
        start = first

        @pl.loop(0, size)
        def _(i):
            staged[start + i] = acc[start + i].astype(jnp.bfloat16)

        copies.append(
            pltpu.make_async_copy(staged.at[pl.ds(start, size)], outs[k], out_sems.at[k])
        )
        copies[-1].start()
        first += size
    for copy in copies:
        copy.wait()


def tile_sum(adjacency, live, take, put, sources, out_sizes, transposed):
    slots, tile = adjacency.shape[1], adjacency.shape[2]
    width = sources[0].shape[-1]
    sources = [s.reshape(-1, tile, width) for s in sources]
    src_sizes = [s.shape[0] for s in sources]
    anywhere = pl.BlockSpec(memory_space=pltpu.HBM)
    scalars = pl.BlockSpec(memory_space=pltpu.SMEM)
    return pl.pallas_call(
        functools.partial(tile_kernel, transposed, src_sizes, out_sizes),
        in_specs=[scalars] * 3 + [anywhere] * (1 + len(sources)),
        out_specs=[anywhere] * len(out_sizes),
        scratch_shapes=[
            pltpu.VMEM((slots, tile, tile), jnp.bfloat16),
            pltpu.VMEM((sum(src_sizes), tile, width), jnp.bfloat16),
            pltpu.VMEM((sum(out_sizes), tile, width), jnp.float32),
            pltpu.VMEM((sum(out_sizes), tile, width), jnp.bfloat16),
            pltpu.SemaphoreType.DMA((slots // GROUP,)),
            pltpu.SemaphoreType.DMA((len(sources),)),
            pltpu.SemaphoreType.DMA((len(out_sizes),)),
        ],
        out_shape=[
            jax.ShapeDtypeStruct((size, tile, width), jnp.bfloat16)
            for size in out_sizes
        ],
        compiler_params=pltpu.CompilerParams(vmem_limit_bytes=VMEM_LIMIT),
        cost_estimate=pl.CostEstimate(
            flops=2 * slots * tile * tile * width,
            bytes_accessed=slots * tile * tile * 2,
            transcendentals=0,
        ),
    )(live, take, put, adjacency, *sources)


def split_dot(exact, other, dims):
    high = exact.astype(jnp.bfloat16)
    low = (exact - high.astype(jnp.float32)).astype(jnp.bfloat16)
    dot = functools.partial(
        lax.dot_general, dimension_numbers=dims, preferred_element_type=jnp.float32
    )
    return dot(high, other) + dot(low, other)


def middle_kernel(count, *refs):
    weight, bias, cotangent, out, grad, total_out, pre_out = refs[count:]
    total = refs[0][...].astype(jnp.float32)
    for piece in refs[1:count]:
        total += piece[...].astype(jnp.float32)
    shifted = split_dot(total, weight[...], (((1,), (0,)), ((), ()))) + bias[...]
    tanh_term = jnp.tanh(GELU_ROOT * (shifted + GELU_CUBIC * shifted * shifted * shifted))
    out[...] = (0.5 * shifted * (1.0 + tanh_term)).astype(jnp.bfloat16)
    slope = 0.5 * (1.0 + tanh_term) + 0.5 * shifted * (
        1.0 - tanh_term * tanh_term
    ) * GELU_ROOT * (1.0 + 3.0 * GELU_CUBIC * shifted * shifted)
    pre_grad = cotangent[...].astype(jnp.float32) * slope
    grad[...] = pre_grad.astype(jnp.bfloat16)
    total_out[...] = total
    pre_out[...] = pre_grad


def middle(pieces, weight, bias, cotangent):
    rows, width = cotangent.shape
    vmem = pl.BlockSpec(memory_space=pltpu.VMEM)
    return pl.pallas_call(
        functools.partial(middle_kernel, len(pieces)),
        in_specs=[vmem] * (len(pieces) + 3),
        out_specs=[vmem] * 4,
        out_shape=[jax.ShapeDtypeStruct((rows, width), jnp.bfloat16)] * 2
        + [jax.ShapeDtypeStruct((rows, width), jnp.float32)] * 2,
        compiler_params=pltpu.CompilerParams(vmem_limit_bytes=VMEM_LIMIT),
    )(*pieces, weight, bias.reshape(1, width), cotangent)


def load_kernel(total, pre_grad, load):
    width = total.shape[1]
    rows = (((0,), (0,)), ((), ()))
    rounded = pre_grad[...].astype(jnp.bfloat16)
    load[:, :width] = split_dot(total[...], rounded, rows)
    ones = jnp.ones((total.shape[0], LANES), jnp.bfloat16)
    load[:, width:] = split_dot(pre_grad[...], ones, rows)


def loads(total, pre_grad):
    width = total.shape[1]
    vmem = pl.BlockSpec(memory_space=pltpu.VMEM)
    return pl.pallas_call(
        load_kernel,
        in_specs=[vmem] * 2,
        out_specs=vmem,
        out_shape=jax.ShapeDtypeStruct((width, width + LANES), jnp.float32),
        compiler_params=pltpu.CompilerParams(vmem_limit_bytes=VMEM_LIMIT),
    )(total, pre_grad)


def last_kernel(pieces, weight, out, held, sems):
    copies = [
        pltpu.make_async_copy(pieces.at[k], held.at[k], sems.at[k])
        for k in range(held.shape[0])
    ]
    for copy in copies:
        copy.start()
    total = jnp.zeros(out.shape, jnp.float32)
    for k, copy in enumerate(copies):
        copy.wait()
        total += held[k].astype(jnp.float32)
    out[...] = lax.dot_general(
        total.astype(jnp.bfloat16),
        weight[...],
        (((1,), (1,)), ((), ())),
        preferred_element_type=jnp.float32,
    ).astype(jnp.bfloat16)


def last(pieces, weight):
    _, rows, width = pieces.shape
    vmem = pl.BlockSpec(memory_space=pltpu.VMEM)
    return pl.pallas_call(
        last_kernel,
        in_specs=[pl.BlockSpec(memory_space=pltpu.HBM), vmem],
        out_specs=vmem,
        out_shape=jax.ShapeDtypeStruct((rows, width), jnp.bfloat16),
        scratch_shapes=[
            pltpu.VMEM(pieces.shape, jnp.bfloat16),
            pltpu.SemaphoreType.DMA((pieces.shape[0],)),
        ],
        compiler_params=pltpu.CompilerParams(vmem_limit_bytes=VMEM_LIMIT),
    )(pieces, weight)


def merge(pieces):
    return sum((p.astype(jnp.float32) for p in pieces[1:]), pieces[0].astype(jnp.float32)).astype(
        jnp.bfloat16
    )


def shards(features, cotangent, weight, bias, adjacency, tile_rows, tile_cols, live_tiles):
    vertices, width = features.shape
    tile = adjacency.shape[2]
    scale = 1.0 / math.sqrt(vertices * N_ROW * N_COL)
    live = live_tiles.reshape(1)
    row_id, col_id = lax.axis_index("row"), lax.axis_index("col")
    my_x, my_zl = row_id // N_ZL, row_id % N_ZL
    my_zh, my_y, my_core = col_id // 8, col_id // 2 % 4, col_id % 2

    per = vertices // tile
    r, c = tile_rows[0], tile_cols[0]
    rc, cc = r // per, c // per
    c_x, c_zl = cc // 2, cc % 2
    r_zh, r_y, r_core = rc // 8, rc // 2 % 4, rc % 2
    half = (r_core ^ my_core) * 16
    ahead = (r_zh - my_zh) & 3
    part = ((ahead == 3) | (ahead == 0)).astype(jnp.int32)
    place = ((ahead == 1) | (ahead == 0)).astype(jnp.int32)
    put_rows = (half + part * 8 + ((r_y - my_y) & 3) * 2 + place) * per + r % per
    take_cols = (((my_x - c_x) & 3) * 2 + (c_zl ^ my_zl)) * per + c % per
    take_rows = (half + ((my_y - r_y) & 3) * 4 + ((my_zh - r_zh) & 3)) * per + r % per

    moves = [(dx, dzl) for dx in range(N_X) for dzl in range(N_ZL)]
    with jax.named_scope("gather_features"):
        sources = [features] + [row_shift(features, *m) for m in moves[1:]]
    with jax.named_scope("tiles_forward"):
        parts = tile_sum(
            adjacency, live, take_cols, put_rows, sources, [8 * per] * 4, False
        )
    with jax.named_scope("sum_over_col"):
        others = [col_shift(send, dcore=1) for send in parts[2:]]

        def over_y(keep, other, first, size):
            added = []
            for k in range(N_Y):
                rows = slice(2 * per * k + first * per, 2 * per * k + (first + size) * per)
                added.append(merge([keep[rows], other[rows]]))
            return [added[0]] + [col_shift(added[k], dy=k) for k in (2, 1, 3)]

        both = over_y(parts[0], others[0], 0, 2)
        far = col_shift(merge([p[:per] for p in both]), dzh=2)
        near = col_shift(merge([p[per:] for p in both]), dzh=1)
        back = over_y(parts[1], others[1], 0, 1)
        *back, near, others[1] = lax.optimization_barrier((*back, near, others[1]))
        pieces = over_y(parts[1], others[1], 1, 1) + [far, near, col_shift(merge(back), dzh=3)]
        pieces = [p.reshape(vertices, width) for p in pieces]
    with jax.named_scope("pointwise"):
        layer_out, grad, total, pre_grad = middle(pieces, weight, bias, cotangent)
    with jax.named_scope("gather_gradients"):
        near = [col_shift(grad, dzh=k) for k in range(1, N_ZH)]
        load = loads(total, pre_grad).reshape(N_COL, -1, width + LANES)
        *near, load = lax.optimization_barrier((*near, load))
        here = [jnp.concatenate([grad] + near)]
    with jax.named_scope("sum_weight_grad"):
        load = jnp.sum(lax.all_to_all(load, "col", 0, 0, tiled=True), axis=0)
        load = jnp.broadcast_to(load, (N_ROW,) + load.shape)
        load = jnp.sum(lax.all_to_all(load, "row", 0, 0, tiled=True), axis=0) * scale
    with jax.named_scope("gather_gradients"):
        here += [col_shift(here[0], dy=k) for k in range(1, N_Y)]
        there = [col_shift(p, dcore=1) for p in here]
    with jax.named_scope("tiles_backward"):
        (back,) = tile_sum(adjacency, live, take_rows, c, here + there, [N_ROW * per], True)
    with jax.named_scope("sum_over_row"):
        back = back.reshape(N_ROW, vertices, width)
        back = lax.all_to_all(back, "row", 0, 0, tiled=True)
        features_grad = last(back, weight)
    with jax.named_scope("sum_weight_grad"):
        load = jnp.broadcast_to(load, (N_COL,) + load.shape)
        load = lax.all_to_all(load, "col", 0, 0, tiled=True).reshape(width, -1)
        weight_grad, bias_grad = load[:, :width], load[:, width]
    return layer_out, features_grad, weight_grad, bias_grad


def solution(mesh):
    placed = (
        P(("row", "col"), None),
        P(("row", "col"), None),
        P(),
        P(),
        P("row", "col", None, None),
        P("row", "col"),
        P("row", "col"),
        P("row", "col"),
    )
    return jax.shard_map(
        shards,
        mesh=mesh,
        in_specs=placed,
        out_specs=(P(("row", "col"), None), P(("row", "col"), None), P(), P()),
        check_vma=False,
    )
```

```python
import functools
import math

import jax
import jax.numpy as jnp
from jax import lax
from jax.experimental import pallas as pl
from jax.experimental.pallas import tpu as pltpu
from jax.sharding import PartitionSpec as P

GELU_ROOT = 0.7978845608028654
GELU_CUBIC = 0.044715

N_X, N_ZL, N_ZH, N_Y, N_CORE = 4, 2, 4, 4, 2
N_ROW = N_X * N_ZL
N_COL = N_ZH * N_Y * N_CORE
GROUP = 24
VMEM_LIMIT = 60 * 1024 * 1024
VMEM_MOST = 65408 * 1024
LANES = 128


def row_shift(value, dx, dzl):
    pairs = []
    for i in range(N_ROW):
        x, zl = divmod(i, N_ZL)
        pairs.append((i, (x + dx) % N_X * N_ZL + (zl ^ dzl)))
    return lax.ppermute(value, "row", pairs)


def col_shift(value, dzh=0, dy=0, dcore=0):
    pairs = []
    for i in range(N_COL):
        zh, y, core = i // (N_Y * N_CORE), i // N_CORE % N_Y, i % N_CORE
        pairs.append(
            (i, ((zh + dzh) % N_ZH * N_Y + (y + dy) % N_Y) * N_CORE + (core ^ dcore))
        )
    return lax.ppermute(value, "col", pairs)


def tile_kernel(transposed, src_sizes, out_sizes, live, take, put, tiles, *refs):
    n_src, n_out = len(src_sizes), len(out_sizes)
    sources = refs[:n_src]
    outs = refs[n_src : n_src + n_out]
    held, src, acc, staged, tile_sems, in_sems, out_sems = refs[n_src + n_out :]
    groups = live[0] // GROUP

    def tile_copy(g):
        rows = pl.ds(g * GROUP, GROUP)
        return pltpu.make_async_copy(tiles.at[0, rows], held.at[rows], tile_sems.at[g])

    copies, first = [], 0
    for k, size in enumerate(src_sizes):
        copies.append(
            pltpu.make_async_copy(sources[k], src.at[pl.ds(first, size)], in_sems.at[k])
        )
        first += size
    for copy in copies:
        copy.start()

    @pl.loop(0, groups)
    def _(g):
        tile_copy(g).start()

    @pl.loop(0, acc.shape[0])
    def _(i):
        acc[i] = jnp.zeros(acc.shape[1:], jnp.float32)

    for copy in copies:
        copy.wait()

    @pl.loop(0, groups)
    def _(g):
        tile_copy(g).wait()

        for j in range(GROUP):
            slot = g * GROUP + j
            product = lax.dot_general(
                held[slot],
                src[take[slot]],
                (((0 if transposed else 1,), (0,)), ((), ())),
                preferred_element_type=jnp.float32,
            )
            acc[put[slot]] += product

    copies, first = [], 0
    for k, size in enumerate(out_sizes):
        start = first

        @pl.loop(0, size)
        def _(i):
            staged[start + i] = acc[start + i].astype(jnp.bfloat16)

        copies.append(
            pltpu.make_async_copy(staged.at[pl.ds(start, size)], outs[k], out_sems.at[k])
        )
        copies[-1].start()
        first += size
    for copy in copies:
        copy.wait()


def tile_sum(adjacency, live, take, put, sources, out_sizes, transposed, vmem):
    slots, tile = adjacency.shape[1], adjacency.shape[2]
    width = sources[0].shape[-1]
    sources = [s.reshape(-1, tile, width) for s in sources]
    src_sizes = [s.shape[0] for s in sources]
    anywhere = pl.BlockSpec(memory_space=pltpu.HBM)
    scalars = pl.BlockSpec(memory_space=pltpu.SMEM)
    return pl.pallas_call(
        functools.partial(tile_kernel, transposed, src_sizes, out_sizes),
        in_specs=[scalars] * 3 + [anywhere] * (1 + len(sources)),
        out_specs=[anywhere] * len(out_sizes),
        scratch_shapes=[
            pltpu.VMEM((slots, tile, tile), jnp.bfloat16),
            pltpu.VMEM((sum(src_sizes), tile, width), jnp.bfloat16),
            pltpu.VMEM((sum(out_sizes), tile, width), jnp.float32),
            pltpu.VMEM((sum(out_sizes), tile, width), jnp.bfloat16),
            pltpu.SemaphoreType.DMA((slots // GROUP,)),
            pltpu.SemaphoreType.DMA((len(sources),)),
            pltpu.SemaphoreType.DMA((len(out_sizes),)),
        ],
        out_shape=[
            jax.ShapeDtypeStruct((size, tile, width), jnp.bfloat16)
            for size in out_sizes
        ],
        compiler_params=pltpu.CompilerParams(vmem_limit_bytes=vmem),
        cost_estimate=pl.CostEstimate(
            flops=2 * slots * tile * tile * width,
            bytes_accessed=slots * tile * tile * 2,
            transcendentals=0,
        ),
    )(live, take, put, adjacency, *sources)


def split_dot(exact, other, dims):
    high = exact.astype(jnp.bfloat16)
    low = (exact - high.astype(jnp.float32)).astype(jnp.bfloat16)
    dot = functools.partial(
        lax.dot_general, dimension_numbers=dims, preferred_element_type=jnp.float32
    )
    return dot(high, other) + dot(low, other)


def middle_kernel(count, *refs):
    weight, bias, cotangent, out, grad, total_out, pre_out = refs[count:]
    total = refs[0][...].astype(jnp.float32)
    for piece in refs[1:count]:
        total += piece[...].astype(jnp.float32)
    shifted = split_dot(total, weight[...], (((1,), (0,)), ((), ()))) + bias[...]
    tanh_term = jnp.tanh(GELU_ROOT * (shifted + GELU_CUBIC * shifted * shifted * shifted))
    out[...] = (0.5 * shifted * (1.0 + tanh_term)).astype(jnp.bfloat16)
    slope = 0.5 * (1.0 + tanh_term) + 0.5 * shifted * (
        1.0 - tanh_term * tanh_term
    ) * GELU_ROOT * (1.0 + 3.0 * GELU_CUBIC * shifted * shifted)
    pre_grad = cotangent[...].astype(jnp.float32) * slope
    grad[...] = pre_grad.astype(jnp.bfloat16)
    total_out[...] = total
    pre_out[...] = pre_grad


def middle(pieces, weight, bias, cotangent):
    rows, width = cotangent.shape
    vmem = pl.BlockSpec(memory_space=pltpu.VMEM)
    return pl.pallas_call(
        functools.partial(middle_kernel, len(pieces)),
        in_specs=[vmem] * (len(pieces) + 3),
        out_specs=[vmem] * 4,
        out_shape=[jax.ShapeDtypeStruct((rows, width), jnp.bfloat16)] * 2
        + [jax.ShapeDtypeStruct((rows, width), jnp.float32)] * 2,
        compiler_params=pltpu.CompilerParams(vmem_limit_bytes=VMEM_LIMIT),
    )(*pieces, weight, bias.reshape(1, width), cotangent)


def load_kernel(total, pre_grad, load):
    width = total.shape[1]
    rows = (((0,), (0,)), ((), ()))
    rounded = pre_grad[...].astype(jnp.bfloat16)
    load[:, :width] = split_dot(total[...], rounded, rows)
    ones = jnp.ones((total.shape[0], LANES), jnp.bfloat16)
    load[:, width:] = split_dot(pre_grad[...], ones, rows)


def loads(total, pre_grad):
    width = total.shape[1]
    vmem = pl.BlockSpec(memory_space=pltpu.VMEM)
    return pl.pallas_call(
        load_kernel,
        in_specs=[vmem] * 2,
        out_specs=vmem,
        out_shape=jax.ShapeDtypeStruct((width, width + LANES), jnp.float32),
        compiler_params=pltpu.CompilerParams(vmem_limit_bytes=VMEM_LIMIT),
    )(total, pre_grad)


def last_kernel(pieces, weight, out):
    total = pieces[0].astype(jnp.float32)
    for k in range(1, pieces.shape[0]):
        total += pieces[k].astype(jnp.float32)
    out[...] = lax.dot_general(
        total.astype(jnp.bfloat16),
        weight[...],
        (((1,), (1,)), ((), ())),
        preferred_element_type=jnp.float32,
    ).astype(jnp.bfloat16)


def last(pieces, weight):
    _, rows, width = pieces.shape
    vmem = pl.BlockSpec(memory_space=pltpu.VMEM)
    return pl.pallas_call(
        last_kernel,
        in_specs=[vmem] * 2,
        out_specs=vmem,
        out_shape=jax.ShapeDtypeStruct((rows, width), jnp.bfloat16),
        compiler_params=pltpu.CompilerParams(vmem_limit_bytes=VMEM_LIMIT),
    )(pieces, weight)


def merge(pieces):
    return sum((p.astype(jnp.float32) for p in pieces[1:]), pieces[0].astype(jnp.float32)).astype(
        jnp.bfloat16
    )


def shards(features, cotangent, weight, bias, adjacency, tile_rows, tile_cols, live_tiles):
    vertices, width = features.shape
    tile = adjacency.shape[2]
    scale = 1.0 / math.sqrt(vertices * N_ROW * N_COL)
    live = live_tiles.reshape(1)
    row_id, col_id = lax.axis_index("row"), lax.axis_index("col")
    my_x, my_zl = row_id // N_ZL, row_id % N_ZL
    my_zh, my_y, my_core = col_id // 8, col_id // 2 % 4, col_id % 2

    per = vertices // tile
    r, c = tile_rows[0], tile_cols[0]
    rc, cc = r // per, c // per
    c_x, c_zl = cc // 2, cc % 2
    r_zh, r_y, r_core = rc // 8, rc // 2 % 4, rc % 2
    half = (r_core ^ my_core) * 16
    ahead = (r_zh - my_zh) & 3
    part = ((ahead == 3) | (ahead == 0)).astype(jnp.int32)
    place = ((ahead == 1) | (ahead == 0)).astype(jnp.int32)
    put_rows = (half + part * 8 + ((r_y - my_y) & 3) * 2 + place) * per + r % per
    take_cols = (((my_x - c_x) & 3) * 2 + (c_zl ^ my_zl)) * per + c % per
    take_rows = (half + ((my_y - r_y) & 3) * 4 + ((my_zh - r_zh) & 3)) * per + r % per

    moves = [(dx, dzl) for dx in range(N_X) for dzl in range(N_ZL)]
    with jax.named_scope("gather_features"):
        sources = [features] + [row_shift(features, *m) for m in moves[1:]]
    with jax.named_scope("tiles_forward"):
        parts = tile_sum(
            adjacency, live, take_cols, put_rows, sources, [8 * per] * 4, False, VMEM_MOST
        )
    with jax.named_scope("sum_over_col"):
        sums, pieces = [], []
        for keep, send in zip(parts[:2], parts[2:]):
            other = col_shift(send, dcore=1)
            cut = [slice(2 * per * k, 2 * per * (k + 1)) for k in range(N_Y)]
            added = [merge([keep[s], other[s]]) for s in cut]
            arrived = [added[0]] + [col_shift(added[k], dy=k) for k in (2, 1, 3)]
            if pieces:
                *arrived, pieces[1] = lax.optimization_barrier((*arrived, pieces[1]))
            sums = [merge([p[:per] for p in arrived]), merge([p[per:] for p in arrived])]
            if not pieces:
                pieces = [col_shift(sums[0], dzh=2), col_shift(sums[1], dzh=1)]
            else:
                pieces += [col_shift(sums[0], dzh=3), sums[1]]
        pieces = [p.reshape(vertices, width) for p in pieces]
    with jax.named_scope("pointwise"):
        layer_out, grad, total, pre_grad = middle(pieces, weight, bias, cotangent)
    with jax.named_scope("gather_gradients"):
        near = [col_shift(grad, dzh=k) for k in range(1, N_ZH)]
        load = loads(total, pre_grad).reshape(N_COL, -1, width + LANES)
        *near, load = lax.optimization_barrier((*near, load))
        here = [jnp.concatenate([grad] + near)]
    with jax.named_scope("sum_weight_grad"):
        load = jnp.sum(lax.all_to_all(load, "col", 0, 0, tiled=True), axis=0)
        load = jnp.broadcast_to(load, (N_ROW,) + load.shape)
        load = jnp.sum(lax.all_to_all(load, "row", 0, 0, tiled=True), axis=0) * scale
    with jax.named_scope("gather_gradients"):
        here += [col_shift(here[0], dy=k) for k in range(1, N_Y)]
        *here, load = lax.optimization_barrier((*here, load))
        there = [col_shift(p, dcore=1) for p in here]
        *there, load = lax.optimization_barrier((*there, load))
    with jax.named_scope("tiles_backward"):
        (back,) = tile_sum(
            adjacency, live, take_rows, c, here + there, [N_ROW * per], True, VMEM_LIMIT
        )
    with jax.named_scope("sum_over_row"):
        back = back.reshape(N_ROW, vertices, width)
        back = lax.all_to_all(back, "row", 0, 0, tiled=True)
        features_grad = last(back, weight)
    with jax.named_scope("sum_weight_grad"):
        load = jnp.broadcast_to(load, (N_COL,) + load.shape)
        load = lax.all_to_all(load, "col", 0, 0, tiled=True).reshape(width, -1)
        weight_grad, bias_grad = load[:, :width], load[:, width]
    return layer_out, features_grad, weight_grad, bias_grad


def solution(mesh):
    placed = (
        P(("row", "col"), None),
        P(("row", "col"), None),
        P(),
        P(),
        P("row", "col", None, None),
        P("row", "col"),
        P("row", "col"),
        P("row", "col"),
    )
    return jax.shard_map(
        shards,
        mesh=mesh,
        in_specs=placed,
        out_specs=(P(("row", "col"), None), P(("row", "col"), None), P(), P()),
        check_vma=False,
    )
```

```python
import functools
import math

import jax
import jax.numpy as jnp
from jax import lax
from jax.experimental import pallas as pl
from jax.experimental.pallas import tpu as pltpu
from jax.sharding import PartitionSpec as P

GELU_ROOT = 0.7978845608028654
GELU_CUBIC = 0.044715

N_X, N_ZL, N_ZH, N_Y, N_CORE = 4, 2, 4, 4, 2
N_ROW = N_X * N_ZL
N_COL = N_ZH * N_Y * N_CORE
PIECE = 8
GROUP = 24
VMEM_LIMIT = 60 * 1024 * 1024
VMEM_MOST = 65408 * 1024
LANES = 128


def row_shift(value, dx, dzl):
    pairs = []
    for i in range(N_ROW):
        x, zl = divmod(i, N_ZL)
        pairs.append((i, (x + dx) % N_X * N_ZL + (zl ^ dzl)))
    return lax.ppermute(value, "row", pairs)


def col_shift(value, dzh=0, dy=0, dcore=0):
    pairs = []
    for i in range(N_COL):
        zh, y, core = i // (N_Y * N_CORE), i // N_CORE % N_Y, i % N_CORE
        pairs.append(
            (i, ((zh + dzh) % N_ZH * N_Y + (y + dy) % N_Y) * N_CORE + (core ^ dcore))
        )
    return lax.ppermute(value, "col", pairs)


def tile_kernel(transposed, src_sizes, out_sizes, live, take, put, tiles, *refs):
    n_src, n_out = len(src_sizes), len(out_sizes)
    sources = refs[:n_src]
    outs = refs[n_src : n_src + n_out]
    held, src, acc, staged, tile_sems, in_sems, out_sems = refs[n_src + n_out :]
    groups = live[0] // GROUP

    def tile_copy(g):
        rows = pl.ds(g * GROUP, GROUP)
        return pltpu.make_async_copy(tiles.at[0, rows], held.at[rows], tile_sems.at[g])

    copies, first = [], 0
    for k, size in enumerate(src_sizes):
        copies.append(
            pltpu.make_async_copy(sources[k], src.at[pl.ds(first, size)], in_sems.at[k])
        )
        first += size
    for copy in copies:
        copy.start()

    @pl.loop(0, groups)
    def _(g):
        tile_copy(g).start()

    @pl.loop(0, acc.shape[0] // 4)
    def _(i):
        for j in range(4):
            acc[i * 4 + j] = jnp.zeros(acc.shape[1:], jnp.float32)

    for copy in copies:
        copy.wait()

    def product(slot):
        value = lax.dot_general(
            held[slot],
            src[take[slot]],
            (((0 if transposed else 1,), (0,)), ((), ())),
            preferred_element_type=jnp.float32,
        )
        acc[put[slot]] += value

    @pl.loop(0, groups // 2)
    def _(g):
        tile_copy(2 * g).wait()
        tile_copy(2 * g + 1).wait()
        for j in range(2 * GROUP):
            product(2 * g * GROUP + j)

    @pl.when(groups % 2 == 1)
    def _():
        tile_copy(groups - 1).wait()
        for j in range(GROUP):
            product((groups - 1) * GROUP + j)

    copies, first = [], 0
    for k, size in enumerate(out_sizes):
        for part in range(0, size, PIECE):
            start = first + part

            @pl.loop(0, PIECE // 4)
            def _(i):
                for j in range(4):
                    row = start + i * 4 + j
                    staged[row] = acc[row].astype(jnp.bfloat16)

            copies.append(
                pltpu.make_async_copy(
                    staged.at[pl.ds(start, PIECE)],
                    outs[k].at[pl.ds(part, PIECE)],
                    out_sems.at[start // PIECE],
                )
            )
            copies[-1].start()
        first += size
    for copy in copies:
        copy.wait()


def tile_sum(adjacency, live, take, put, sources, out_sizes, transposed, vmem):
    slots, tile = adjacency.shape[1], adjacency.shape[2]
    width = sources[0].shape[-1]
    sources = [s.reshape(-1, tile, width) for s in sources]
    src_sizes = [s.shape[0] for s in sources]
    anywhere = pl.BlockSpec(memory_space=pltpu.HBM)
    scalars = pl.BlockSpec(memory_space=pltpu.SMEM)
    return pl.pallas_call(
        functools.partial(tile_kernel, transposed, src_sizes, out_sizes),
        in_specs=[scalars] * 3 + [anywhere] * (1 + len(sources)),
        out_specs=[anywhere] * len(out_sizes),
        scratch_shapes=[
            pltpu.VMEM((slots, tile, tile), jnp.bfloat16),
            pltpu.VMEM((sum(src_sizes), tile, width), jnp.bfloat16),
            pltpu.VMEM((sum(out_sizes), tile, width), jnp.float32),
            pltpu.VMEM((sum(out_sizes), tile, width), jnp.bfloat16),
            pltpu.SemaphoreType.DMA((slots // GROUP,)),
            pltpu.SemaphoreType.DMA((len(sources),)),
            pltpu.SemaphoreType.DMA((sum(out_sizes) // PIECE,)),
        ],
        out_shape=[
            jax.ShapeDtypeStruct((size, tile, width), jnp.bfloat16)
            for size in out_sizes
        ],
        compiler_params=pltpu.CompilerParams(vmem_limit_bytes=vmem),
        cost_estimate=pl.CostEstimate(
            flops=2 * slots * tile * tile * width,
            bytes_accessed=slots * tile * tile * 2,
            transcendentals=0,
        ),
    )(live, take, put, adjacency, *sources)


def split_dot(exact, other, dims):
    high = exact.astype(jnp.bfloat16)
    low = (exact - high.astype(jnp.float32)).astype(jnp.bfloat16)
    dot = functools.partial(
        lax.dot_general, dimension_numbers=dims, preferred_element_type=jnp.float32
    )
    return dot(high, other) + dot(low, other)


def middle_kernel(count, *refs):
    weight, bias, cotangent, out, grad, total_out, pre_out = refs[count:]
    total = refs[0][...].astype(jnp.float32)
    for piece in refs[1:count]:
        total += piece[...].astype(jnp.float32)
    shifted = split_dot(total, weight[...], (((1,), (0,)), ((), ()))) + bias[...]
    tanh_term = jnp.tanh(GELU_ROOT * (shifted + GELU_CUBIC * shifted * shifted * shifted))
    out[...] = (0.5 * shifted * (1.0 + tanh_term)).astype(jnp.bfloat16)
    slope = 0.5 * (1.0 + tanh_term) + 0.5 * shifted * (
        1.0 - tanh_term * tanh_term
    ) * GELU_ROOT * (1.0 + 3.0 * GELU_CUBIC * shifted * shifted)
    pre_grad = cotangent[...].astype(jnp.float32) * slope
    grad[...] = pre_grad.astype(jnp.bfloat16)
    total_out[...] = total
    pre_out[...] = pre_grad


def middle(pieces, weight, bias, cotangent):
    rows, width = cotangent.shape
    vmem = pl.BlockSpec(memory_space=pltpu.VMEM)
    return pl.pallas_call(
        functools.partial(middle_kernel, len(pieces)),
        in_specs=[vmem] * (len(pieces) + 3),
        out_specs=[vmem] * 4,
        out_shape=[jax.ShapeDtypeStruct((rows, width), jnp.bfloat16)] * 2
        + [jax.ShapeDtypeStruct((rows, width), jnp.float32)] * 2,
        compiler_params=pltpu.CompilerParams(vmem_limit_bytes=VMEM_LIMIT),
    )(*pieces, weight, bias.reshape(1, width), cotangent)


def load_kernel(total, pre_grad, load):
    width = total.shape[1]
    rows = (((0,), (0,)), ((), ()))
    rounded = pre_grad[...].astype(jnp.bfloat16)
    load[:, :width] = split_dot(total[...], rounded, rows)
    ones = jnp.ones((total.shape[0], LANES), jnp.bfloat16)
    load[:, width:] = split_dot(pre_grad[...], ones, rows)


def loads(total, pre_grad):
    width = total.shape[1]
    vmem = pl.BlockSpec(memory_space=pltpu.VMEM)
    return pl.pallas_call(
        load_kernel,
        in_specs=[vmem] * 2,
        out_specs=vmem,
        out_shape=jax.ShapeDtypeStruct((width, width + LANES), jnp.float32),
        compiler_params=pltpu.CompilerParams(vmem_limit_bytes=VMEM_LIMIT),
    )(total, pre_grad)


def last_kernel(pieces, weight, out):
    total = pieces[0].astype(jnp.float32)
    for k in range(1, pieces.shape[0]):
        total += pieces[k].astype(jnp.float32)
    out[...] = lax.dot_general(
        total.astype(jnp.bfloat16),
        weight[...],
        (((1,), (1,)), ((), ())),
        preferred_element_type=jnp.float32,
    ).astype(jnp.bfloat16)


def last(pieces, weight):
    _, rows, width = pieces.shape
    vmem = pl.BlockSpec(memory_space=pltpu.VMEM)
    return pl.pallas_call(
        last_kernel,
        in_specs=[vmem] * 2,
        out_specs=vmem,
        out_shape=jax.ShapeDtypeStruct((rows, width), jnp.bfloat16),
        compiler_params=pltpu.CompilerParams(vmem_limit_bytes=VMEM_LIMIT),
    )(pieces, weight)


def merge(pieces):
    return sum((p.astype(jnp.float32) for p in pieces[1:]), pieces[0].astype(jnp.float32)).astype(
        jnp.bfloat16
    )


def shards(features, cotangent, weight, bias, adjacency, tile_rows, tile_cols, live_tiles):
    vertices, width = features.shape
    tile = adjacency.shape[2]
    scale = 1.0 / math.sqrt(vertices * N_ROW * N_COL)
    live = live_tiles.reshape(1)
    row_id, col_id = lax.axis_index("row"), lax.axis_index("col")
    my_x, my_zl = row_id // N_ZL, row_id % N_ZL
    my_zh, my_y, my_core = col_id // 8, col_id // 2 % 4, col_id % 2

    per = vertices // tile
    r, c = tile_rows[0], tile_cols[0]
    rc, cc = r // per, c // per
    c_x, c_zl = cc // 2, cc % 2
    r_zh, r_y, r_core = rc // 8, rc // 2 % 4, rc % 2
    half = (r_core ^ my_core) * 16
    ahead = (r_zh - my_zh) & 3
    part = ((ahead == 3) | (ahead == 0)).astype(jnp.int32)
    place = ((ahead == 1) | (ahead == 0)).astype(jnp.int32)
    put_rows = (half + part * 8 + ((r_y - my_y) & 3) * 2 + place) * per + r % per
    take_cols = (((my_x - c_x) & 3) * 2 + (c_zl ^ my_zl)) * per + c % per
    take_rows = (half + ((my_y - r_y) & 3) * 4 + ((my_zh - r_zh) & 3)) * per + r % per

    moves = [(dx, dzl) for dx in range(N_X) for dzl in range(N_ZL)]
    with jax.named_scope("gather_features"):
        sources = [features] + [row_shift(features, *m) for m in moves[1:]]
    with jax.named_scope("tiles_forward"):
        parts = tile_sum(
            adjacency, live, take_cols, put_rows, sources, [8 * per] * 4, False, VMEM_MOST
        )
    with jax.named_scope("sum_over_col"):
        sums, pieces = [], []
        for keep, send in zip(parts[:2], parts[2:]):
            other = col_shift(send, dcore=1)
            cut = [slice(2 * per * k, 2 * per * (k + 1)) for k in range(N_Y)]
            added = [merge([keep[s], other[s]]) for s in cut]
            arrived = [added[0]] + [col_shift(added[k], dy=k) for k in (2, 1, 3)]
            if pieces:
                *arrived, pieces[1] = lax.optimization_barrier((*arrived, pieces[1]))
            sums = [merge([p[:per] for p in arrived]), merge([p[per:] for p in arrived])]
            if not pieces:
                pieces = [col_shift(sums[0], dzh=2), col_shift(sums[1], dzh=1)]
            else:
                pieces += [col_shift(sums[0], dzh=3), sums[1]]
        pieces = [p.reshape(vertices, width) for p in pieces]
    with jax.named_scope("pointwise"):
        layer_out, grad, total, pre_grad = middle(pieces, weight, bias, cotangent)
    with jax.named_scope("gather_gradients"):
        near = [col_shift(grad, dzh=k) for k in range(1, N_ZH)]
        load = loads(total, pre_grad).reshape(N_COL, -1, width + LANES)
        *near, load = lax.optimization_barrier((*near, load))
        here = [jnp.concatenate([grad] + near)]
    with jax.named_scope("sum_weight_grad"):
        load = jnp.sum(lax.all_to_all(load, "col", 0, 0, tiled=True), axis=0)
        load = jnp.broadcast_to(load, (N_ROW,) + load.shape)
        load = jnp.sum(lax.all_to_all(load, "row", 0, 0, tiled=True), axis=0) * scale
    with jax.named_scope("gather_gradients"):
        here += [col_shift(here[0], dy=k) for k in range(1, N_Y)]
        there = [col_shift(p, dcore=1) for p in here]
    with jax.named_scope("tiles_backward"):
        (back,) = tile_sum(
            adjacency, live, take_rows, c, here + there, [N_ROW * per], True, VMEM_LIMIT
        )
    with jax.named_scope("sum_over_row"):
        back = back.reshape(N_ROW, vertices, width)
        back = lax.all_to_all(back, "row", 0, 0, tiled=True)
        features_grad = last(back, weight)
    with jax.named_scope("sum_weight_grad"):
        load = jnp.broadcast_to(load, (N_COL,) + load.shape)
        load = lax.all_to_all(load, "col", 0, 0, tiled=True).reshape(width, -1)
        weight_grad, bias_grad = load[:, :width], load[:, width]
    return layer_out, features_grad, weight_grad, bias_grad


def solution(mesh):
    placed = (
        P(("row", "col"), None),
        P(("row", "col"), None),
        P(),
        P(),
        P("row", "col", None, None),
        P("row", "col"),
        P("row", "col"),
        P("row", "col"),
    )
    return jax.shard_map(
        shards,
        mesh=mesh,
        in_specs=placed,
        out_specs=(P(("row", "col"), None), P(("row", "col"), None), P(), P()),
        check_vma=False,
    )
```

```python
import functools
import math

import jax
import jax.numpy as jnp
from jax import lax
from jax.experimental import pallas as pl
from jax.experimental.pallas import tpu as pltpu
from jax.sharding import PartitionSpec as P

GELU_ROOT = 0.7978845608028654
GELU_CUBIC = 0.044715

N_X, N_ZL, N_ZH, N_Y, N_CORE = 4, 2, 4, 4, 2
N_ROW = N_X * N_ZL
N_COL = N_ZH * N_Y * N_CORE
PIECE = 8
GROUP = 24
VMEM_LIMIT = 60 * 1024 * 1024
VMEM_MOST = 65408 * 1024
LANES = 128


def row_shift(value, dx, dzl):
    pairs = []
    for i in range(N_ROW):
        x, zl = divmod(i, N_ZL)
        pairs.append((i, (x + dx) % N_X * N_ZL + (zl ^ dzl)))
    return lax.ppermute(value, "row", pairs)


def col_shift(value, dzh=0, dy=0, dcore=0):
    pairs = []
    for i in range(N_COL):
        zh, y, core = i // (N_Y * N_CORE), i // N_CORE % N_Y, i % N_CORE
        pairs.append(
            (i, ((zh + dzh) % N_ZH * N_Y + (y + dy) % N_Y) * N_CORE + (core ^ dcore))
        )
    return lax.ppermute(value, "col", pairs)


def tile_kernel(transposed, src_sizes, out_sizes, live, take, put, tiles, *refs):
    n_src, n_out = len(src_sizes), len(out_sizes)
    sources = refs[:n_src]
    outs = refs[n_src : n_src + n_out]
    held, src, acc, staged, tile_sems, in_sems, out_sems = refs[n_src + n_out :]
    groups = live[0] // GROUP

    def tile_copy(g):
        rows = pl.ds(g * GROUP, GROUP)
        return pltpu.make_async_copy(tiles.at[0, rows], held.at[rows], tile_sems.at[g])

    copies, first = [], 0
    for k, size in enumerate(src_sizes):
        copies.append(
            pltpu.make_async_copy(sources[k], src.at[pl.ds(first, size)], in_sems.at[k])
        )
        first += size
    for copy in copies:
        copy.start()

    @pl.loop(0, groups)
    def _(g):
        tile_copy(g).start()

    @pl.loop(0, acc.shape[0] // 4)
    def _(i):
        for j in range(4):
            acc[i * 4 + j] = jnp.zeros(acc.shape[1:], jnp.float32)

    for copy in copies:
        copy.wait()

    def product(slot):
        value = lax.dot_general(
            held[slot],
            src[take[slot]],
            (((0 if transposed else 1,), (0,)), ((), ())),
            preferred_element_type=jnp.float32,
        )
        acc[put[slot]] += value

    @pl.loop(0, groups // 2)
    def _(g):
        tile_copy(2 * g).wait()
        tile_copy(2 * g + 1).wait()
        for j in range(2 * GROUP):
            product(2 * g * GROUP + j)

    @pl.when(groups % 2 == 1)
    def _():
        tile_copy(groups - 1).wait()
        for j in range(GROUP):
            product((groups - 1) * GROUP + j)

    copies, first = [], 0
    for k, size in enumerate(out_sizes):
        for part in range(0, size, PIECE):
            start = first + part

            @pl.loop(0, PIECE // 4)
            def _(i):
                for j in range(4):
                    row = start + i * 4 + j
                    staged[row] = acc[row].astype(jnp.bfloat16)

            copies.append(
                pltpu.make_async_copy(
                    staged.at[pl.ds(start, PIECE)],
                    outs[k].at[pl.ds(part, PIECE)],
                    out_sems.at[start // PIECE],
                )
            )
            copies[-1].start()
        first += size
    for copy in copies:
        copy.wait()


def tile_sum(adjacency, live, take, put, sources, out_sizes, transposed, vmem):
    slots, tile = adjacency.shape[1], adjacency.shape[2]
    width = sources[0].shape[-1]
    sources = [s.reshape(-1, tile, width) for s in sources]
    src_sizes = [s.shape[0] for s in sources]
    anywhere = pl.BlockSpec(memory_space=pltpu.HBM)
    scalars = pl.BlockSpec(memory_space=pltpu.SMEM)
    return pl.pallas_call(
        functools.partial(tile_kernel, transposed, src_sizes, out_sizes),
        in_specs=[scalars] * 3 + [anywhere] * (1 + len(sources)),
        out_specs=[anywhere] * len(out_sizes),
        scratch_shapes=[
            pltpu.VMEM((slots, tile, tile), jnp.bfloat16),
            pltpu.VMEM((sum(src_sizes), tile, width), jnp.bfloat16),
            pltpu.VMEM((sum(out_sizes), tile, width), jnp.float32),
            pltpu.VMEM((sum(out_sizes), tile, width), jnp.bfloat16),
            pltpu.SemaphoreType.DMA((slots // GROUP,)),
            pltpu.SemaphoreType.DMA((len(sources),)),
            pltpu.SemaphoreType.DMA((sum(out_sizes) // PIECE,)),
        ],
        out_shape=[
            jax.ShapeDtypeStruct((size, tile, width), jnp.bfloat16)
            for size in out_sizes
        ],
        compiler_params=pltpu.CompilerParams(vmem_limit_bytes=vmem),
        cost_estimate=pl.CostEstimate(
            flops=2 * slots * tile * tile * width,
            bytes_accessed=slots * tile * tile * 2,
            transcendentals=0,
        ),
    )(live, take, put, adjacency, *sources)


def split_dot(exact, other, dims):
    high = exact.astype(jnp.bfloat16)
    low = (exact - high.astype(jnp.float32)).astype(jnp.bfloat16)
    dot = functools.partial(
        lax.dot_general, dimension_numbers=dims, preferred_element_type=jnp.float32
    )
    return dot(high, other) + dot(low, other)


def middle_kernel(count, *refs):
    weight, bias, cotangent, out, grad, total_out, pre_out = refs[count:]
    total = refs[0][...].astype(jnp.float32)
    for piece in refs[1:count]:
        total += piece[...].astype(jnp.float32)
    shifted = split_dot(total, weight[...], (((1,), (0,)), ((), ()))) + bias[...]
    tanh_term = jnp.tanh(GELU_ROOT * (shifted + GELU_CUBIC * shifted * shifted * shifted))
    out[...] = (0.5 * shifted * (1.0 + tanh_term)).astype(jnp.bfloat16)
    slope = 0.5 * (1.0 + tanh_term) + 0.5 * shifted * (
        1.0 - tanh_term * tanh_term
    ) * GELU_ROOT * (1.0 + 3.0 * GELU_CUBIC * shifted * shifted)
    pre_grad = cotangent[...].astype(jnp.float32) * slope
    grad[...] = pre_grad.astype(jnp.bfloat16)
    total_out[...] = total
    pre_out[...] = pre_grad


def middle(pieces, weight, bias, cotangent):
    rows, width = cotangent.shape
    vmem = pl.BlockSpec(memory_space=pltpu.VMEM)
    return pl.pallas_call(
        functools.partial(middle_kernel, len(pieces)),
        in_specs=[vmem] * (len(pieces) + 3),
        out_specs=[vmem] * 4,
        out_shape=[jax.ShapeDtypeStruct((rows, width), jnp.bfloat16)] * 2
        + [jax.ShapeDtypeStruct((rows, width), jnp.float32)] * 2,
        compiler_params=pltpu.CompilerParams(vmem_limit_bytes=VMEM_LIMIT),
    )(*pieces, weight, bias.reshape(1, width), cotangent)


def load_kernel(total, pre_grad, load):
    width = total.shape[1]
    rows = (((0,), (0,)), ((), ()))
    rounded = pre_grad[...].astype(jnp.bfloat16)
    load[:, :width] = split_dot(total[...], rounded, rows).astype(load.dtype)
    ones = jnp.ones((total.shape[0], LANES), jnp.bfloat16)
    load[:, width:] = split_dot(pre_grad[...], ones, rows).astype(load.dtype)


def loads(total, pre_grad):
    width = total.shape[1]
    vmem = pl.BlockSpec(memory_space=pltpu.VMEM)
    return pl.pallas_call(
        load_kernel,
        in_specs=[vmem] * 2,
        out_specs=vmem,
        out_shape=jax.ShapeDtypeStruct((width, width + LANES), jnp.bfloat16),
        compiler_params=pltpu.CompilerParams(vmem_limit_bytes=VMEM_LIMIT),
    )(total, pre_grad)


def last_kernel(pieces, weight, out):
    total = pieces[0].astype(jnp.float32)
    for k in range(1, pieces.shape[0]):
        total += pieces[k].astype(jnp.float32)
    out[...] = lax.dot_general(
        total.astype(jnp.bfloat16),
        weight[...],
        (((1,), (1,)), ((), ())),
        preferred_element_type=jnp.float32,
    ).astype(jnp.bfloat16)


def last(pieces, weight):
    _, rows, width = pieces.shape
    vmem = pl.BlockSpec(memory_space=pltpu.VMEM)
    return pl.pallas_call(
        last_kernel,
        in_specs=[vmem] * 2,
        out_specs=vmem,
        out_shape=jax.ShapeDtypeStruct((rows, width), jnp.bfloat16),
        compiler_params=pltpu.CompilerParams(vmem_limit_bytes=VMEM_LIMIT),
    )(pieces, weight)


def merge(pieces):
    return sum((p.astype(jnp.float32) for p in pieces[1:]), pieces[0].astype(jnp.float32)).astype(
        jnp.bfloat16
    )


def shards(features, cotangent, weight, bias, adjacency, tile_rows, tile_cols, live_tiles):
    vertices, width = features.shape
    tile = adjacency.shape[2]
    scale = 1.0 / math.sqrt(vertices * N_ROW * N_COL)
    live = live_tiles.reshape(1)
    row_id, col_id = lax.axis_index("row"), lax.axis_index("col")
    my_x, my_zl = row_id // N_ZL, row_id % N_ZL
    my_zh, my_y, my_core = col_id // 8, col_id // 2 % 4, col_id % 2

    per = vertices // tile
    r, c = tile_rows[0], tile_cols[0]
    rc, cc = r // per, c // per
    c_x, c_zl = cc // 2, cc % 2
    r_zh, r_y, r_core = rc // 8, rc // 2 % 4, rc % 2
    half = (r_core ^ my_core) * 16
    ahead = (r_zh - my_zh) & 3
    part = ((ahead == 3) | (ahead == 0)).astype(jnp.int32)
    place = ((ahead == 1) | (ahead == 0)).astype(jnp.int32)
    put_rows = (half + part * 8 + ((r_y - my_y) & 3) * 2 + place) * per + r % per
    take_cols = (((my_x - c_x) & 3) * 2 + (c_zl ^ my_zl)) * per + c % per
    take_rows = (half + ((my_y - r_y) & 3) * 4 + ((my_zh - r_zh) & 3)) * per + r % per

    moves = [(dx, dzl) for dx in range(N_X) for dzl in range(N_ZL)]
    with jax.named_scope("gather_features"):
        sources = [features] + [row_shift(features, *m) for m in moves[1:]]
    with jax.named_scope("tiles_forward"):
        parts = tile_sum(
            adjacency, live, take_cols, put_rows, sources, [8 * per] * 4, False, VMEM_MOST
        )
    with jax.named_scope("sum_over_col"):
        sums, pieces = [], []
        for keep, send in zip(parts[:2], parts[2:]):
            other = col_shift(send, dcore=1)
            cut = [slice(2 * per * k, 2 * per * (k + 1)) for k in range(N_Y)]
            added = [merge([keep[s], other[s]]) for s in cut]
            arrived = [added[0]] + [col_shift(added[k], dy=k) for k in (2, 1, 3)]
            if pieces:
                *arrived, pieces[1] = lax.optimization_barrier((*arrived, pieces[1]))
            sums = [merge([p[:per] for p in arrived]), merge([p[per:] for p in arrived])]
            if not pieces:
                pieces = [col_shift(sums[0], dzh=2), col_shift(sums[1], dzh=1)]
            else:
                pieces += [col_shift(sums[0], dzh=3), sums[1]]
        pieces = [p.reshape(vertices, width) for p in pieces]
    with jax.named_scope("pointwise"):
        layer_out, grad, total, pre_grad = middle(pieces, weight, bias, cotangent)
    with jax.named_scope("gather_gradients"):
        near = [col_shift(grad, dzh=k) for k in range(1, N_ZH)]
        load = loads(total, pre_grad).reshape(N_COL, -1, width + LANES)
        *near, load = lax.optimization_barrier((*near, load))
        here = [jnp.concatenate([grad] + near)]
    with jax.named_scope("sum_weight_grad"):
        load = lax.all_to_all(load, "col", 0, 0, tiled=True)
        load = jnp.sum(load.astype(jnp.float32), axis=0)
        there = [col_shift(here[0], dcore=1)]
        there[0], load = lax.optimization_barrier((there[0], load))
        load = jnp.broadcast_to(load, (N_ROW,) + load.shape)
        load = jnp.sum(lax.all_to_all(load, "row", 0, 0, tiled=True), axis=0) * scale
    with jax.named_scope("gather_gradients"):
        here += [col_shift(here[0], dy=k) for k in range(1, N_Y)]
        there += [col_shift(p, dcore=1) for p in here[1:]]
    with jax.named_scope("tiles_backward"):
        (back,) = tile_sum(
            adjacency, live, take_rows, c, here + there, [N_ROW * per], True, VMEM_LIMIT
        )
    with jax.named_scope("sum_over_row"):
        back = back.reshape(N_ROW, vertices, width)
        back = lax.all_to_all(back, "row", 0, 0, tiled=True)
        features_grad = last(back, weight)
    with jax.named_scope("sum_weight_grad"):
        load = jnp.broadcast_to(load, (N_COL,) + load.shape)
        load = lax.all_to_all(load, "col", 0, 0, tiled=True).reshape(width, -1)
        weight_grad, bias_grad = load[:, :width], load[:, width]
    return layer_out, features_grad, weight_grad, bias_grad


def solution(mesh):
    placed = (
        P(("row", "col"), None),
        P(("row", "col"), None),
        P(),
        P(),
        P("row", "col", None, None),
        P("row", "col"),
        P("row", "col"),
        P("row", "col"),
    )
    return jax.shard_map(
        shards,
        mesh=mesh,
        in_specs=placed,
        out_specs=(P(("row", "col"), None), P(("row", "col"), None), P(), P()),
        check_vma=False,
    )
```

```python
import functools
import math

import jax
import jax.numpy as jnp
from jax import lax
from jax.experimental import pallas as pl
from jax.experimental.pallas import tpu as pltpu
from jax.sharding import PartitionSpec as P

GELU_ROOT = 0.7978845608028654
GELU_CUBIC = 0.044715

N_X, N_ZL, N_ZH, N_Y, N_CORE = 4, 2, 4, 4, 2
N_ROW = N_X * N_ZL
N_COL = N_ZH * N_Y * N_CORE
PIECE = 8
GROUP = 24
VMEM_LIMIT = 60 * 1024 * 1024
VMEM_MOST = 65408 * 1024
LANES = 128


def row_shift(value, dx, dzl):
    pairs = []
    for i in range(N_ROW):
        x, zl = divmod(i, N_ZL)
        pairs.append((i, (x + dx) % N_X * N_ZL + (zl ^ dzl)))
    return lax.ppermute(value, "row", pairs)


def col_shift(value, dzh=0, dy=0, dcore=0):
    pairs = []
    for i in range(N_COL):
        zh, y, core = i // (N_Y * N_CORE), i // N_CORE % N_Y, i % N_CORE
        pairs.append(
            (i, ((zh + dzh) % N_ZH * N_Y + (y + dy) % N_Y) * N_CORE + (core ^ dcore))
        )
    return lax.ppermute(value, "col", pairs)


def tile_kernel(transposed, src_sizes, out_sizes, live, take, put, tiles, *refs):
    n_src, n_out = len(src_sizes), len(out_sizes)
    sources = refs[:n_src]
    outs = refs[n_src : n_src + n_out]
    held, src, acc, staged, tile_sems, in_sems, out_sems = refs[n_src + n_out :]
    groups = live[0] // GROUP

    def tile_copy(g):
        rows = pl.ds(g * GROUP, GROUP)
        return pltpu.make_async_copy(tiles.at[0, rows], held.at[rows], tile_sems.at[g])

    copies, first = [], 0
    for k, size in enumerate(src_sizes):
        copies.append(
            pltpu.make_async_copy(sources[k], src.at[pl.ds(first, size)], in_sems.at[k])
        )
        first += size
    for copy in copies:
        copy.start()

    @pl.loop(0, groups)
    def _(g):
        tile_copy(g).start()

    @pl.loop(0, acc.shape[0] // 4)
    def _(i):
        for j in range(4):
            acc[i * 4 + j] = jnp.zeros(acc.shape[1:], jnp.float32)

    for copy in copies:
        copy.wait()

    def product(slot):
        value = lax.dot_general(
            held[slot],
            src[take[slot]],
            (((0 if transposed else 1,), (0,)), ((), ())),
            preferred_element_type=jnp.float32,
        )
        acc[put[slot]] += value

    @pl.loop(0, groups // 2)
    def _(g):
        tile_copy(2 * g).wait()
        tile_copy(2 * g + 1).wait()
        for j in range(2 * GROUP):
            product(2 * g * GROUP + j)

    @pl.when(groups % 2 == 1)
    def _():
        tile_copy(groups - 1).wait()
        for j in range(GROUP):
            product((groups - 1) * GROUP + j)

    copies, first = [], 0
    for k, size in enumerate(out_sizes):
        for part in range(0, size, PIECE):
            start = first + part

            @pl.loop(0, PIECE // 4)
            def _(i):
                for j in range(4):
                    row = start + i * 4 + j
                    staged[row] = acc[row].astype(jnp.bfloat16)

            copies.append(
                pltpu.make_async_copy(
                    staged.at[pl.ds(start, PIECE)],
                    outs[k].at[pl.ds(part, PIECE)],
                    out_sems.at[start // PIECE],
                )
            )
            copies[-1].start()
        first += size
    for copy in copies:
        copy.wait()


def tile_sum(adjacency, live, take, put, sources, out_sizes, transposed, vmem):
    slots, tile = adjacency.shape[1], adjacency.shape[2]
    width = sources[0].shape[-1]
    sources = [s.reshape(-1, tile, width) for s in sources]
    src_sizes = [s.shape[0] for s in sources]
    anywhere = pl.BlockSpec(memory_space=pltpu.HBM)
    scalars = pl.BlockSpec(memory_space=pltpu.SMEM)
    return pl.pallas_call(
        functools.partial(tile_kernel, transposed, src_sizes, out_sizes),
        in_specs=[scalars] * 3 + [anywhere] * (1 + len(sources)),
        out_specs=[anywhere] * len(out_sizes),
        scratch_shapes=[
            pltpu.VMEM((slots, tile, tile), jnp.bfloat16),
            pltpu.VMEM((sum(src_sizes), tile, width), jnp.bfloat16),
            pltpu.VMEM((sum(out_sizes), tile, width), jnp.float32),
            pltpu.VMEM((sum(out_sizes), tile, width), jnp.bfloat16),
            pltpu.SemaphoreType.DMA((slots // GROUP,)),
            pltpu.SemaphoreType.DMA((len(sources),)),
            pltpu.SemaphoreType.DMA((sum(out_sizes) // PIECE,)),
        ],
        out_shape=[
            jax.ShapeDtypeStruct((size, tile, width), jnp.bfloat16)
            for size in out_sizes
        ],
        compiler_params=pltpu.CompilerParams(vmem_limit_bytes=vmem),
        cost_estimate=pl.CostEstimate(
            flops=2 * slots * tile * tile * width,
            bytes_accessed=slots * tile * tile * 2,
            transcendentals=0,
        ),
    )(live, take, put, adjacency, *sources)


def split_dot(exact, other, dims):
    high = exact.astype(jnp.bfloat16)
    low = (exact - high.astype(jnp.float32)).astype(jnp.bfloat16)
    dot = functools.partial(
        lax.dot_general, dimension_numbers=dims, preferred_element_type=jnp.float32
    )
    return dot(high, other) + dot(low, other)


def middle_kernel(count, *refs):
    weight, bias, cotangent, out, grad, total_out, pre_out = refs[count:]
    total = refs[0][...].astype(jnp.float32)
    for piece in refs[1:count]:
        total += piece[...].astype(jnp.float32)
    shifted = split_dot(total, weight[...], (((1,), (0,)), ((), ()))) + bias[...]
    tanh_term = jnp.tanh(GELU_ROOT * (shifted + GELU_CUBIC * shifted * shifted * shifted))
    out[...] = (0.5 * shifted * (1.0 + tanh_term)).astype(jnp.bfloat16)
    slope = 0.5 * (1.0 + tanh_term) + 0.5 * shifted * (
        1.0 - tanh_term * tanh_term
    ) * GELU_ROOT * (1.0 + 3.0 * GELU_CUBIC * shifted * shifted)
    pre_grad = cotangent[...].astype(jnp.float32) * slope
    grad[...] = pre_grad.astype(jnp.bfloat16)
    total_out[...] = total
    pre_out[...] = pre_grad


def middle(pieces, weight, bias, cotangent):
    rows, width = cotangent.shape
    vmem = pl.BlockSpec(memory_space=pltpu.VMEM)
    return pl.pallas_call(
        functools.partial(middle_kernel, len(pieces)),
        in_specs=[vmem] * (len(pieces) + 3),
        out_specs=[vmem] * 4,
        out_shape=[jax.ShapeDtypeStruct((rows, width), jnp.bfloat16)] * 2
        + [jax.ShapeDtypeStruct((rows, width), jnp.float32)] * 2,
        compiler_params=pltpu.CompilerParams(vmem_limit_bytes=VMEM_LIMIT),
    )(*pieces, weight, bias.reshape(1, width), cotangent)


def load_kernel(total, pre_grad, load):
    width = total.shape[1]
    rows = (((0,), (0,)), ((), ()))
    rounded = pre_grad[...].astype(jnp.bfloat16)
    load[:, :width] = split_dot(total[...], rounded, rows).astype(load.dtype)
    ones = jnp.ones((total.shape[0], LANES), jnp.bfloat16)
    load[:, width:] = split_dot(pre_grad[...], ones, rows).astype(load.dtype)


def loads(total, pre_grad):
    width = total.shape[1]
    vmem = pl.BlockSpec(memory_space=pltpu.VMEM)
    return pl.pallas_call(
        load_kernel,
        in_specs=[vmem] * 2,
        out_specs=vmem,
        out_shape=jax.ShapeDtypeStruct((width, width + LANES), jnp.bfloat16),
        compiler_params=pltpu.CompilerParams(vmem_limit_bytes=VMEM_LIMIT),
    )(total, pre_grad)


def last_kernel(pieces, weight, out):
    total = pieces[0].astype(jnp.float32)
    for k in range(1, pieces.shape[0]):
        total += pieces[k].astype(jnp.float32)
    out[...] = lax.dot_general(
        total.astype(jnp.bfloat16),
        weight[...],
        (((1,), (1,)), ((), ())),
        preferred_element_type=jnp.float32,
    ).astype(jnp.bfloat16)


def last(pieces, weight):
    _, rows, width = pieces.shape
    vmem = pl.BlockSpec(memory_space=pltpu.VMEM)
    return pl.pallas_call(
        last_kernel,
        in_specs=[vmem] * 2,
        out_specs=vmem,
        out_shape=jax.ShapeDtypeStruct((rows, width), jnp.bfloat16),
        compiler_params=pltpu.CompilerParams(vmem_limit_bytes=VMEM_LIMIT),
    )(pieces, weight)


def merge(pieces):
    return sum((p.astype(jnp.float32) for p in pieces[1:]), pieces[0].astype(jnp.float32)).astype(
        jnp.bfloat16
    )


def shards(features, cotangent, weight, bias, adjacency, tile_rows, tile_cols, live_tiles):
    vertices, width = features.shape
    tile = adjacency.shape[2]
    scale = 1.0 / math.sqrt(vertices * N_ROW * N_COL)
    live = live_tiles.reshape(1)
    row_id, col_id = lax.axis_index("row"), lax.axis_index("col")
    my_x, my_zl = row_id // N_ZL, row_id % N_ZL
    my_zh, my_y, my_core = col_id // 8, col_id // 2 % 4, col_id % 2

    per = vertices // tile
    r, c = tile_rows[0], tile_cols[0]
    rc, cc = r // per, c // per
    c_x, c_zl = cc // 2, cc % 2
    r_zh, r_y, r_core = rc // 8, rc // 2 % 4, rc % 2
    half = (r_core ^ my_core) * 16
    ahead = (r_zh - my_zh) & 3
    part = ((ahead == 3) | (ahead == 0)).astype(jnp.int32)
    place = ((ahead == 1) | (ahead == 0)).astype(jnp.int32)
    put_rows = (half + part * 8 + ((r_y - my_y) & 3) * 2 + place) * per + r % per
    take_cols = (((my_x - c_x) & 3) * 2 + (c_zl ^ my_zl)) * per + c % per
    take_rows = (half + ((my_y - r_y) & 3) * 4 + ((my_zh - r_zh) & 3)) * per + r % per

    moves = [(dx, dzl) for dx in range(N_X) for dzl in range(N_ZL)]
    with jax.named_scope("gather_features"):
        sources = [features] + [row_shift(features, *m) for m in moves[1:]]
    with jax.named_scope("tiles_forward"):
        parts = tile_sum(
            adjacency, live, take_cols, put_rows, sources, [8 * per] * 4, False, VMEM_MOST
        )
    with jax.named_scope("sum_over_col"):
        sums, pieces = [], []
        for keep, send in zip(parts[:2], parts[2:]):
            other = col_shift(send, dcore=1)
            cut = [slice(2 * per * k, 2 * per * (k + 1)) for k in range(N_Y)]
            added = [merge([keep[s], other[s]]) for s in cut]
            arrived = [added[0]] + [col_shift(added[k], dy=k) for k in (2, 1, 3)]
            if pieces:
                *arrived, pieces[1] = lax.optimization_barrier((*arrived, pieces[1]))
            sums = [merge([p[:per] for p in arrived]), merge([p[per:] for p in arrived])]
            if not pieces:
                pieces = [col_shift(sums[0], dzh=2), col_shift(sums[1], dzh=1)]
            else:
                pieces += [col_shift(sums[0], dzh=3), sums[1]]
        pieces = [p.reshape(vertices, width) for p in pieces]
    with jax.named_scope("pointwise"):
        layer_out, grad, total, pre_grad = middle(pieces, weight, bias, cotangent)
    with jax.named_scope("gather_gradients"):
        near = [col_shift(grad, dzh=k) for k in range(1, N_ZH)]
        load = loads(total, pre_grad).reshape(N_COL, -1, width + LANES)
        *near, load = lax.optimization_barrier((*near, load))
        here = [jnp.concatenate([grad] + near)]
    with jax.named_scope("sum_weight_grad"):
        load = lax.all_to_all(load, "col", 0, 0, tiled=True)
        load = jnp.sum(load.astype(jnp.float32), axis=0)
        load = jnp.broadcast_to(load, (N_ROW,) + load.shape)
        load = jnp.sum(lax.all_to_all(load, "row", 0, 0, tiled=True), axis=0) * scale
    with jax.named_scope("gather_gradients"):
        here += [col_shift(here[0], dy=k) for k in range(1, N_Y)]
        there = [col_shift(p, dcore=1) for p in here]
    with jax.named_scope("tiles_backward"):
        (back,) = tile_sum(
            adjacency, live, take_rows, c, here + there, [N_ROW * per], True, VMEM_LIMIT
        )
    with jax.named_scope("sum_over_row"):
        back = back.reshape(N_ROW, vertices, width)
        back = lax.all_to_all(back, "row", 0, 0, tiled=True)
        features_grad = last(back, weight)
    with jax.named_scope("sum_weight_grad"):
        load = jnp.broadcast_to(load, (N_COL,) + load.shape)
        load = lax.all_to_all(load, "col", 0, 0, tiled=True).reshape(width, -1)
        weight_grad, bias_grad = load[:, :width], load[:, width]
    return layer_out, features_grad, weight_grad, bias_grad


def solution(mesh):
    placed = (
        P(("row", "col"), None),
        P(("row", "col"), None),
        P(),
        P(),
        P("row", "col", None, None),
        P("row", "col"),
        P("row", "col"),
        P("row", "col"),
    )
    return jax.shard_map(
        shards,
        mesh=mesh,
        in_specs=placed,
        out_specs=(P(("row", "col"), None), P(("row", "col"), None), P(), P()),
        check_vma=False,
    )
```
